128 devices in a mesh: expert: 16 (over x, z_lo, core), tensor: 8 (over z_hi, y).
Axes of the slice: x: 4, y: 4, z: 4 (z_hi: 2, z_lo: 2; z = z_hi * 2 + z_lo), core: 2. Of those that a mesh axis runs over, the one named last changes fastest.
Arguments:
- learner_delta: bfloat16 [128, 56, 16, 1024], P(('expert', 'tensor')), may hold values from -3 to 3
- owner_block: int32 [128], replicated, may hold values from 0 to 127, each once
- expert_shadow: float32 [16, 7168, 1024], P('expert', None, 'tensor'), may hold values from -10 to 10, as said below
- tile_mode: int32 [16, 56, 8], P('expert', None, 'tensor'), may hold values from 0 to 1
- attn_delta: bfloat16 [512, 16384], P(('expert', 'tensor')), may hold values from -3 to 3
- attn_shadow: float32 [512, 16384], P(None, 'tensor'), may hold values from -10 to 10, as said below
Outputs:
- expert_new: float32 [16, 7168, 1024], P('expert', None, 'tensor')
- expert_codes: bfloat16 [16, 7168, 1024], P('expert', None, 'tensor')
- expert_amax: float32 [16, 56, 1024], P('expert', None, 'tensor')
- attn_new: float32 [512, 16384], P(None, 'tensor')
- attn_codes: bfloat16 [512, 16384], P(None, 'tensor')
- attn_amax: float32 [4, 128], P(None, 'tensor')
The draws below stay inside these ranges and needn't reach their ends.
Inputs may be any that keep to these rules, and one draw needn't show every extreme that they name: `owner_block`: each row block number appears once. `expert_shadow`: finite real weights. `attn_shadow`: finite real weights.
All inputs are finite; a program needn't handle non-finite values.
Results may differ from the reference program's by a relative error of at most 0.001.
Values may be sent and summed in bfloat16 or wider, within the bound.
A program may use at most 128 MiB of HBM per device.

```python
import math
import jax
import jax.numpy as jnp

D = 7168
F = 1024
KV_RANK = 512
KV_COLS = 16384
BLK = 128
EXPERTS = 16
RB = 56
DEVICES = 128


def scaled_field(key, count_rows, count_cols, base, reach_ratio):
    first, second = jax.random.split(key, 2)
    row_scale = jnp.exp(jax.random.uniform(first, (count_rows, 1), jnp.float32) * math.log(reach_ratio))
    col_scale = jnp.exp(jax.random.uniform(second, (1, count_cols), jnp.float32) * math.log(reach_ratio))
    return 0.02 * base * row_scale * col_scale


def draw_expert_shadow(key, part):
    key = jax.random.fold_in(key, 11)
    first, second = jax.random.split(key, 2)
    base = jnp.clip(jax.random.normal(first, (EXPERTS, D, F), jnp.float32), -5.0, 5.0)
    return scaled_field(second, D, F, base, 10.0)


def draw_attn_shadow(key, part):
    key = jax.random.fold_in(key, 23)
    first, second = jax.random.split(key, 2)
    base = jnp.clip(jax.random.normal(first, (KV_RANK, KV_COLS), jnp.float32), -5.0, 5.0)
    return scaled_field(second, KV_RANK, KV_COLS, base, 10.0)


def place_ends(values, rng, least, largest):
    spot = [jax.random.randint(jax.random.fold_in(rng, axis), (), 0, length) for axis, length in enumerate(values.shape)]
    longest = values.shape.index(max(values.shape))
    beside = spot[:longest] + [(spot[longest] + 1) % values.shape[longest]] + spot[longest + 1:]
    return values.at[tuple(spot)].set(least).at[tuple(beside)].set(largest)


def shard_levels(stream_key, dims, cuts, low, largest):
    loudness, own = 1.0, jax.random.fold_in(stream_key, 6)
    for position, blocks in cuts:
        heights = jnp.exp(jax.random.uniform(jax.random.fold_in(own, position), (blocks,), jnp.float32, low / len(cuts), largest / len(cuts)))
        loudness = loudness * jnp.repeat(heights, dims[position] // blocks).reshape([-1 if axis == position else 1 for axis in range(len(dims))])
    return loudness


def gaussian(key, extent, scale, limit, cuts=(), dtype=jnp.bfloat16):
    level = shard_levels(key, extent, cuts, -0.22, 0.18) if cuts else 1.0
    entries = jax.random.normal(key, extent, jnp.float32) * scale * level
    return jnp.minimum(jnp.maximum(entries, -limit), limit).astype(dtype)


def setup_inputs(seed: int = 0) -> dict:
    key_of = jax.random.split(jax.random.key(seed), 7)
    learner_delta = gaussian(key_of[0], (DEVICES, RB, EXPERTS, F), 0.2, 3.0, ((0, 128),))
    owner_block = jax.random.permutation(key_of[1], DEVICES).astype(jnp.int32)
    expert_shadow = draw_expert_shadow(jax.random.fold_in(key_of[6], 71), 0)
    tile_mode = place_ends(jax.random.randint(key_of[3], (EXPERTS, D // BLK, F // BLK), 0, 2), jax.random.fold_in(key_of[3], 1), 0, 1).astype(jnp.int32)
    attn_delta = gaussian(key_of[4], (KV_RANK, KV_COLS), 0.2, 3.0, ((0, 128),))
    attn_shadow = draw_attn_shadow(jax.random.fold_in(key_of[6], 71), 0)
    return {"learner_delta": learner_delta, "owner_block": owner_block, "expert_shadow": expert_shadow, "tile_mode": tile_mode, "attn_delta": attn_delta, "attn_shadow": attn_shadow}


def expert_quantize(updated, tile_mode):
    magnitude = jnp.abs(updated)
    count_lead = updated.shape[0]
    count_rows = updated.shape[1]
    count_cols = updated.shape[2]
    column_max = magnitude.reshape(count_lead, count_rows // BLK, BLK, count_cols).max(axis=2)
    tile_max = column_max.reshape(count_lead, count_rows // BLK, count_cols // BLK, BLK).max(axis=3)
    tile_wide = jnp.repeat(tile_max, BLK, axis=2)
    mode_wide = jnp.repeat(tile_mode, BLK, axis=2)
    chosen = jnp.where(mode_wide == 0, tile_wide, column_max)
    codes = (updated / (jnp.repeat(chosen, BLK, axis=1) + 1e-6)).astype(jnp.bfloat16)
    return codes, chosen


def attention_quantize(updated):
    count_rows = updated.shape[0]
    count_cols = updated.shape[1]
    tile_max = jnp.abs(updated).reshape(count_rows // BLK, BLK, count_cols // BLK, BLK).max(axis=(1, 3))
    spread_max = jnp.repeat(jnp.repeat(tile_max, BLK, axis=0), BLK, axis=1)
    codes = (updated / (spread_max + 1e-6)).astype(jnp.bfloat16)
    return codes, tile_max


def reference(learner_delta, owner_block, expert_shadow, tile_mode, attn_delta, attn_shadow):
    ordered = jnp.zeros_like(learner_delta).at[owner_block.astype(jnp.int32)].set(learner_delta)
    delta = jnp.transpose(ordered, (2, 0, 1, 3)).reshape(EXPERTS, D, F)
    expert_new = expert_shadow + delta.astype(jnp.float32)
    expert_codes, expert_amax = expert_quantize(expert_new, tile_mode)
    attn_new = attn_shadow + attn_delta.astype(jnp.float32)
    attn_codes, attn_amax = attention_quantize(attn_new)
    return (expert_new, expert_codes, expert_amax, attn_new, attn_codes, attn_amax)
```

```python
import functools

import jax
import jax.numpy as jnp
from jax import lax
from jax.experimental import pallas as pl
from jax.experimental.pallas import tpu as pltpu
from jax.sharding import PartitionSpec as P

MESH = pl.DeviceIdType.MESH
BLK = 128
F32 = jnp.float32
BF16 = jnp.bfloat16

OWNERS = 128
RB = 56
EXPERTS = 16
SHARES = 8
ROWS = OWNERS * RB
ATT_ROWS = 4
ATT_COLS = 2048
ATT_TILES = ATT_COLS // BLK
SUPER = 8
BLOCKS = 16
TILES = 7


def peer_at(e, t, k):
    s = lax.rem(k * 37, 128)
    x = lax.rem(e // 4 + s // 32, 4)
    y = lax.rem(lax.rem(t, 4) + lax.rem(s // 8, 4), 4)
    z = lax.rem((t // 4) * 2 + lax.rem(e // 2, 2) + lax.rem(s // 2, 4), 4)
    c = lax.rem(lax.rem(e, 2) + lax.rem(s, 2), 2)
    return x * 4 + lax.rem(z, 2) * 2 + c, (z // 2) * 4 + y


def exchange(
    delta, attn_delta, attn_shadow, expert_shadow,
    recv, shadow, attn_new, attn_codes, attn_amax,
    held, wide, send, gath, att_old, att_wide,
    load_sem, send_sem, recv_sem, a_send, a_recv, b_send, b_recv, c_send, c_recv,
):
    e = lax.axis_index("expert")
    t = lax.axis_index("tensor")
    me = e * SHARES + t

    barrier = pltpu.get_barrier_semaphore()

    def greet(k, _):
        p = lax.rem(me + k, OWNERS)
        pl.semaphore_signal(barrier, inc=1, device_id=(p // SHARES, lax.rem(p, SHARES)), device_id_type=MESH)
        return 0

    load_delta = pltpu.make_async_copy(delta.at[0], held, load_sem.at[0])
    load_delta.start()
    lax.fori_loop(1, OWNERS, greet, 0)
    own_rows = pltpu.make_async_copy(
        attn_delta.at[:, pl.ds(pl.multiple_of(t * ATT_COLS, ATT_COLS), ATT_COLS)], gath.at[me], load_sem.at[1]
    )
    own_rows.start()
    load_att = pltpu.make_async_copy(attn_shadow, att_old, load_sem.at[2])
    load_att.start()
    load_exp = pltpu.make_async_copy(expert_shadow.at[0], shadow, load_sem.at[3])
    load_exp.start()

    load_delta.wait()

    def widen(r, _):
        rows = held[r].astype(F32)
        for j in range(SHARES):
            wide[j, pl.ds(pl.multiple_of(r * EXPERTS, EXPERTS), EXPERTS), :] = rows[:, j * BLK:(j + 1) * BLK]
        return 0

    lax.fori_loop(0, RB, widen, 0, unroll=2)

    def block_of(pe, pt):
        return wide[pt, pl.ds(pe, RB, stride=EXPERTS), :].astype(BF16)

    recv[me] = block_of(e, t)

    pl.semaphore_wait(barrier, OWNERS - 1)

    for k in range(1, SHARES):
        q = lax.rem(t + k, SHARES)
        pltpu.make_async_remote_copy(
            src_ref=attn_delta.at[:, pl.ds(pl.multiple_of(q * ATT_COLS, ATT_COLS), ATT_COLS)],
            dst_ref=gath.at[me],
            send_sem=a_send,
            recv_sem=a_recv,
            device_id=(e, q),
            device_id_type=MESH,
        ).start()

    def send_block(k, _):
        pe, pt = peer_at(e, t, k)
        p = pe * SHARES + pt
        send[p] = block_of(pe, pt)
        pltpu.make_async_remote_copy(
            src_ref=send.at[p],
            dst_ref=recv.at[me],
            send_sem=send_sem,
            recv_sem=recv_sem,
            device_id=(pe, pt),
            device_id_type=MESH,
        ).start()
        return 0

    lax.fori_loop(1, 33, send_block, 0)

    own_rows.wait()
    pltpu.make_async_copy(gath.at[pl.ds(0, 7)], gath.at[pl.ds(0, 7)], a_recv).wait()

    core = lax.rem(e, 2)

    def chunk(i):
        return gath.at[pl.ds(pl.multiple_of(i * SHARES, SHARES), SHARES)]

    def to_chip(h):
        return pltpu.make_async_remote_copy(
            src_ref=chunk(e), dst_ref=chunk(e), send_sem=b_send.at[h], recv_sem=b_recv.at[h],
            device_id=(lax.rem(e + 2 * h, EXPERTS), t), device_id_type=MESH,
        )

    def to_core(h):
        src = lax.rem(e + EXPERTS - 2 * h, EXPERTS)
        return pltpu.make_async_remote_copy(
            src_ref=chunk(src), dst_ref=chunk(src), send_sem=c_send.at[h], recv_sem=c_recv.at[h],
            device_id=(e + 1 - 2 * core, t), device_id_type=MESH,
        )

    to_core(0).start()
    for h in range(1, 8):
        to_chip(h).start()

    lax.fori_loop(33, OWNERS, send_block, 0)

    for h in range(1, 8):
        to_chip(h).wait_recv()
        to_core(h).start()
    for h in range(8):
        to_core(h).wait_recv()

    load_att.wait()
    for i in range(OWNERS):
        att_wide[i // 2, (i % 2) * 4:(i % 2) * 4 + 4, :] = gath[i].astype(F32)

    def att_tile_row(i, _):
        tops = []
        for j in range(ATT_TILES):
            cols = slice(j * BLK, (j + 1) * BLK)
            groups = pl.ds(i * 16, 16)
            new = att_old[groups, :, cols] + att_wide[groups, :, cols]
            attn_new[groups, :, cols] = new
            top = jnp.max(jnp.max(jnp.max(jnp.abs(new), axis=0), axis=0, keepdims=True), axis=1, keepdims=True)
            codes = new * (1.0 / (top + 1e-6))[None]
            attn_codes[pl.ds(pl.multiple_of(i * BLK, BLK), BLK), cols] = codes.reshape(BLK, BLK).astype(BF16)
            tops.append(jnp.broadcast_to(top, (1, BLK)))
        lane = lax.broadcasted_iota(jnp.int32, (1, BLK), 1)
        row = jnp.zeros((1, BLK), F32)
        for j in range(ATT_TILES):
            row = jnp.where(lane == j, tops[j], row)
        attn_amax[pl.ds(i, 1), :] = row
        return 0

    lax.fori_loop(0, 4, att_tile_row, 0)

    load_exp.wait()
    pltpu.make_async_copy(gath.at[pl.ds(0, 7)], gath.at[pl.ds(0, 7)], a_send).wait()
    for h in range(1, 8):
        to_chip(h).wait_send()
    for h in range(8):
        to_core(h).wait_send()
    whole = pl.ds(0, OWNERS - 1)
    pltpu.make_async_copy(send.at[whole], send.at[whole], send_sem).wait()
    pltpu.make_async_copy(recv.at[whole], recv.at[whole], recv_sem).wait()


def finish(
    owner, mode, recv, shadow, att_new_v, att_codes_v, att_amax_v,
    expert_new, expert_codes, expert_amax, attn_new, attn_codes, attn_amax,
    place, new_v, codes_v, amax_v, att_small, out_sem, new_sem, codes_sem,
):
    copy_an = pltpu.make_async_copy(att_new_v, attn_new, out_sem.at[0])
    copy_ac = pltpu.make_async_copy(att_codes_v, attn_codes, out_sem.at[1])

    def invert(l, _):
        place[owner[l]] = l
        return 0

    lax.fori_loop(0, OWNERS, invert, 0, unroll=8)

    def group_rows(s):
        return pl.ds(pl.multiple_of(s * (BLOCKS * RB), BLOCKS * RB), BLOCKS * RB)

    def copy_new(s):
        return pltpu.make_async_copy(new_v.at[group_rows(s)], expert_new.at[0, group_rows(s)], new_sem)

    def copy_codes(s):
        return pltpu.make_async_copy(codes_v.at[group_rows(s)], expert_codes.at[0, group_rows(s)], codes_sem)

    def group(s, _):
        for j in range(BLOCKS):
            rows = pl.ds(pl.multiple_of((s * BLOCKS + j) * RB, 8), RB)
            new_v[rows, :] = shadow[rows, :] + recv[place[s * BLOCKS + j]].astype(F32)
        copy_new(s).start()
        for j in range(TILES):
            i = s * TILES + j
            rows = pl.ds(pl.multiple_of(i * BLK, BLK), BLK)
            tile = new_v[rows, :]
            column = jnp.max(jnp.abs(tile), axis=0, keepdims=True)
            top = jnp.max(column, axis=1, keepdims=True)
            chosen = jnp.where(mode[i] == 0, jnp.broadcast_to(top, column.shape), column)
            amax_v[pl.ds(i, 1), :] = chosen
            codes_v[rows, :] = (tile * (1.0 / (chosen + 1e-6))).astype(BF16)
        copy_codes(s).start()
        return 0

    copy_an.start()
    copy_ac.start()
    lax.fori_loop(0, SUPER, group, 0)
    att_small[...] = att_amax_v[:, :ATT_TILES]
    copy_am = pltpu.make_async_copy(amax_v, expert_amax.at[0], out_sem.at[2])
    copy_am.start()
    copy_aa = pltpu.make_async_copy(att_small, attn_amax, out_sem.at[3])
    copy_aa.start()
    copy_an.wait()
    copy_ac.wait()
    copy_am.wait()
    copy_aa.wait()
    pltpu.make_async_copy(new_v, expert_new.at[0], new_sem).wait()
    pltpu.make_async_copy(codes_v, expert_codes.at[0], codes_sem).wait()


def on_device(learner_delta, owner_block, expert_shadow, tile_mode, attn_delta, attn_shadow):
    vmem = pl.BlockSpec(memory_space=pltpu.VMEM)
    hbm = pl.BlockSpec(memory_space=pltpu.HBM)
    smem = pl.BlockSpec(memory_space=pltpu.SMEM)
    dma = pltpu.SemaphoreType.DMA
    shape = jax.ShapeDtypeStruct
    recv, shadow, att_new_v, att_codes_v, att_amax_v = pl.pallas_call(
        exchange,
        name="exchange",
        out_shape=(
            shape((OWNERS, RB, BLK), BF16),
            shape((ROWS, BLK), F32),
            shape((64, 8, ATT_COLS), F32),
            shape((512, ATT_COLS), BF16),
            shape((4, BLK), F32),
        ),
        in_specs=[hbm] * 4,
        out_specs=(vmem,) * 5,
        scratch_shapes=[
            pltpu.VMEM((RB, EXPERTS, 1024), BF16),
            pltpu.VMEM((SHARES, RB * EXPERTS, BLK), F32),
            pltpu.VMEM((OWNERS, RB, BLK), BF16),
            pltpu.VMEM((OWNERS, ATT_ROWS, ATT_COLS), BF16),
            pltpu.VMEM((64, 8, ATT_COLS), F32),
            pltpu.VMEM((64, 8, ATT_COLS), F32),
            dma((4,)), dma(()), dma(()), dma(()), dma(()),
            dma((8,)), dma((8,)), dma((8,)), dma((8,)),
        ],
        compiler_params=pltpu.CompilerParams(
            collective_id=0, has_side_effects=True, vmem_limit_bytes=40 << 20
        ),
    )(learner_delta, attn_delta, attn_shadow.reshape(64, 8, ATT_COLS), expert_shadow)

    return pl.pallas_call(
        finish,
        name="finish",
        out_shape=(
            shape((1, ROWS, BLK), F32),
            shape((1, ROWS, BLK), BF16),
            shape((1, ROWS // BLK, BLK), F32),
            shape((512, ATT_COLS), F32),
            shape((512, ATT_COLS), BF16),
            shape((4, ATT_TILES), F32),
        ),
        in_specs=[smem, smem] + [vmem] * 5,
        out_specs=(hbm,) * 6,
        scratch_shapes=[
            pltpu.SMEM((OWNERS,), jnp.int32),
            pltpu.VMEM((ROWS, BLK), F32),
            pltpu.VMEM((ROWS, BLK), BF16),
            pltpu.VMEM((ROWS // BLK, BLK), F32),
            pltpu.VMEM((4, ATT_TILES), F32),
            dma((4,)), dma(()), dma(()),
        ],
        compiler_params=pltpu.CompilerParams(vmem_limit_bytes=40 << 20),
    )(owner_block, tile_mode.reshape(ROWS // BLK), recv, shadow, att_new_v.reshape(512, ATT_COLS), att_codes_v, att_amax_v)


def solution(mesh):
    return jax.shard_map(
        on_device,
        mesh=mesh,
        in_specs=(
            P(("expert", "tensor"), None, None, None),
            P(),
            P("expert", None, "tensor"),
            P("expert", None, "tensor"),
            P(("expert", "tensor"), None),
            P(None, "tensor"),
        ),
        out_specs=(
            P("expert", None, "tensor"),
            P("expert", None, "tensor"),
            P("expert", None, "tensor"),
            P(None, "tensor"),
            P(None, "tensor"),
            P(None, "tensor"),
        ),
        check_vma=False,
    )
```

```python
import functools

import jax
import jax.numpy as jnp
from jax import lax
from jax.experimental import pallas as pl
from jax.experimental.pallas import tpu as pltpu
from jax.sharding import PartitionSpec as P

MESH = pl.DeviceIdType.MESH
BLK = 128
F32 = jnp.float32
BF16 = jnp.bfloat16

OWNERS = 128
RB = 56
EXPERTS = 16
SHARES = 8
ROWS = OWNERS * RB
ATT_ROWS = 4
ATT_COLS = 2048
ATT_TILES = ATT_COLS // BLK
SUPER = 8
BLOCKS = 16
TILES = 7


WIDE_Z = 1024
WIDE_X = ATT_COLS - WIDE_Z
AHEAD, BETWEEN = 40, 3


def hops(s):
    return sum(min(d, 4 - d) for d in (s // 16, s // 4 % 4, s % 4))


TABLE = sorted(((37 * k) % 64 for k in range(64)), key=lambda s: -hops(s))
WORDS = [sum(s << (6 * n) for n, s in enumerate(TABLE[4 * w:4 * w + 4])) for w in range(16)]


def chip_offset(i):
    word = jnp.int32(WORDS[0])
    for w in range(1, 16):
        word = jnp.where(lax.div(i, 4) == w, WORDS[w], word)
    s = lax.rem(word, 64)
    for n in range(1, 4):
        s = jnp.where(lax.rem(i, 4) == n, lax.rem(lax.div(word, 64 ** n), 64), s)
    return lax.div(s, 16), lax.rem(lax.div(s, 4), 4), lax.rem(s, 4)


def exchange(
    delta, attn_delta, attn_shadow, expert_shadow,
    recv, shadow, attn_new, attn_codes, attn_amax,
    held, wide, send, by_z, by_x, other, att_old, att_wide,
    load_sem, send_sem, recv_sem, first_send, first_recv, second_send, second_recv, last_send, last_recv,
):
    e = lax.axis_index("expert")
    t = lax.axis_index("tensor")
    me = e * SHARES + t
    x, y, core = lax.div(e, 4), lax.rem(t, 4), lax.rem(e, 2)
    high, low = lax.div(t, 4), lax.rem(lax.div(e, 2), 2)
    z = high * 2 + low

    def step(v, d):
        return lax.rem(v + d, 4)

    def at(x, y, z, core):
        return x * 4 + lax.rem(z, 2) * 2 + core, lax.div(z, 2) * 4 + y

    load_delta = pltpu.make_async_copy(delta.at[0], held, load_sem.at[0])
    load_delta.start()

    barrier = pltpu.get_barrier_semaphore()
    for de in range(EXPERTS):
        for dt in range(SHARES):
            if de or dt:
                pl.semaphore_signal(
                    barrier, inc=1, device_id=(lax.rem(e + de, EXPERTS), lax.rem(t + dt, SHARES)), device_id_type=MESH
                )

    def columns(high, y, first, count):
        return attn_delta.at[:, pl.ds(pl.multiple_of((high * 4 + y) * ATT_COLS + first, BLK), count)]

    own = (
        pltpu.make_async_copy(columns(high, y, 0, WIDE_Z), by_z.at[core, x, z * 4 + y], load_sem.at[1]),
        pltpu.make_async_copy(columns(1 - high, y, 0, WIDE_Z), other.at[x * 4 + y], load_sem.at[2]),
        pltpu.make_async_copy(columns(high, y, WIDE_Z, WIDE_X), by_x.at[core, x, z * 4 + y], load_sem.at[3]),
    )
    for copy in own:
        copy.start()
    load_att = pltpu.make_async_copy(attn_shadow, att_old, load_sem.at[4])
    load_att.start()
    load_exp = pltpu.make_async_copy(expert_shadow.at[0], shadow, load_sem.at[5])
    load_exp.start()

    load_delta.wait()

    def widen(r, _):
        rows = held[r].astype(F32)
        for j in range(SHARES):
            wide[j, pl.ds(pl.multiple_of(r * EXPERTS, EXPERTS), EXPERTS), :] = rows[:, j * BLK:(j + 1) * BLK]
        return 0

    lax.fori_loop(0, RB, widen, 0, unroll=2)

    def block_of(pe, pt):
        return wide[pt, pl.ds(pe, RB, stride=EXPERTS), :].astype(BF16)

    recv[me] = block_of(e, t)

    pl.semaphore_wait(barrier, OWNERS - 1)

    plane = sorted((k for k in range(1, 16)), key=lambda k: -hops(k))
    for k in plane:
        a, b = k // 4, k % 4
        to = at(step(x, a), step(y, b), z, core)
        for n, (share, dst) in enumerate(((high, by_z.at[core, x, z * 4 + y]), (1 - high, other.at[x * 4 + y]))):
            pltpu.make_async_remote_copy(
                src_ref=columns(share, step(y, b), 0, WIDE_Z), dst_ref=dst,
                send_sem=first_send.at[n], recv_sem=first_recv.at[n], device_id=to, device_id_type=MESH,
            ).start()
        there = step(z, a)
        pltpu.make_async_remote_copy(
            src_ref=columns(lax.div(there, 2), step(y, b), WIDE_Z, WIDE_X), dst_ref=by_x.at[core, x, z * 4 + y],
            send_sem=first_send.at[2], recv_sem=first_recv.at[2],
            device_id=at(x, step(y, b), there, core), device_id_type=MESH,
        ).start()

    def send_block(k, _):
        dx, dy, dz = chip_offset(lax.div(k, 2))
        pe, pt = at(step(x, dx), step(y, dy), step(z, dz), lax.rem(core + 1 - lax.rem(k, 2), 2))
        p = pe * SHARES + pt
        send[p] = block_of(pe, pt)
        pltpu.make_async_remote_copy(
            src_ref=send.at[p],
            dst_ref=recv.at[me],
            send_sem=send_sem,
            recv_sem=recv_sem,
            device_id=(pe, pt),
            device_id_type=MESH,
        ).start()
        return 0

    lax.fori_loop(0, AHEAD, send_block, 0)

    for copy in own:
        copy.wait()
    landed = (by_z.at[0, 0, pl.ds(0, 15)], other.at[pl.ds(0, 15)], by_x.at[0, 0, pl.ds(0, 15)])
    for n, ref in enumerate(landed):
        pltpu.make_async_copy(ref, ref, first_recv.at[n]).wait()

    def along_z(r, d, src=None):
        i, there = step(x, r), step(z, d)
        dst = by_z.at[core, i, pl.ds(z * 4, 4)]
        return pltpu.make_async_remote_copy(
            src_ref=dst if src is None else src, dst_ref=dst,
            send_sem=second_send.at[r, d], recv_sem=second_recv.at[r, d],
            device_id=at(x, y, there, core), device_id_type=MESH,
        )

    def start_z(r, d):
        same = lax.div(step(z, d), 2) == high

        @pl.when(same)
        def _():
            along_z(r, d).start()

        @pl.when(jnp.logical_not(same))
        def _():
            along_z(r, d, other.at[pl.ds(step(x, r) * 4, 4)]).start()

    def along_x(r):
        ref = by_x.at[core, x]
        return pltpu.make_async_remote_copy(
            src_ref=ref, dst_ref=ref, send_sem=second_send.at[r, 0], recv_sem=second_recv.at[r, 0],
            device_id=at(step(x, 4 - r), y, z, core), device_id_type=MESH,
        )

    def across(n, r):
        ref = (by_z, by_x)[n].at[core, step(x, r)]
        return pltpu.make_async_remote_copy(
            src_ref=ref, dst_ref=ref, send_sem=last_send.at[n, r], recv_sem=last_recv.at[n, r],
            device_id=at(x, y, z, 1 - core), device_id_type=MESH,
        )

    starts = []
    for r in range(4):
        starts += [functools.partial(start_z, r, d) for d in (2, 1, 3)]
        if r:
            starts.append(along_x(r).start)
    k = AHEAD
    for start in starts:
        start()
        upto = min(k + BETWEEN, OWNERS - 1)
        if upto > k:
            lax.fori_loop(k, upto, send_block, 0)
            k = upto
    lax.fori_loop(k, OWNERS - 1, send_block, 0)

    def att_widen(m, _):
        i, j = lax.div(m, 4), lax.rem(m, 4)
        gx, gc = lax.div(i, 4), lax.rem(i, 2)
        gz = lax.div(j, 2) * 2 + lax.rem(lax.div(i, 2), 2)
        for n in range(2):
            owner = gz * 4 + lax.rem(j, 2) * 2 + n
            rows = slice(4 * n, 4 * n + 4)
            att_wide[m, rows, :WIDE_Z] = by_z[gc, gx, owner].astype(F32)
            att_wide[m, rows, WIDE_Z:] = by_x[gc, gx, owner].astype(F32)
        return 0

    def att_tile_row(i, _):
        tops = []
        for j in range(ATT_TILES):
            cols = slice(j * BLK, (j + 1) * BLK)
            groups = pl.ds(i * 16, 16)
            new = att_old[groups, :, cols] + att_wide[groups, :, cols]
            attn_new[groups, :, cols] = new
            top = jnp.max(jnp.max(jnp.max(jnp.abs(new), axis=0), axis=0, keepdims=True), axis=1, keepdims=True)
            codes = new * (1.0 / (top + 1e-6))[None]
            attn_codes[pl.ds(pl.multiple_of(i * BLK, BLK), BLK), cols] = codes.reshape(BLK, BLK).astype(BF16)
            tops.append(jnp.broadcast_to(top, (1, BLK)))
        lane = lax.broadcasted_iota(jnp.int32, (1, BLK), 1)
        row = jnp.zeros((1, BLK), F32)
        for j in range(ATT_TILES):
            row = jnp.where(lane == j, tops[j], row)
        attn_amax[pl.ds(i, 1), :] = row
        return 0

    load_att.wait()

    def arrive(r):
        for d in (1, 3, 2):
            along_z(r, d).wait_recv()
        across(0, r).start()
        if r:
            along_x(r).wait_recv()
        across(1, r).start()

    def work(r):
        across(0, r).wait_recv()
        across(1, r).wait_recv()
        i = step(x, r)
        lax.fori_loop(i * 16, i * 16 + 16, att_widen, 0)
        att_tile_row(i, 0)

    for r in range(5):
        if r < 4:
            arrive(r)
        if r:
            work(r - 1)

    load_exp.wait()
    for n, ref in enumerate(landed):
        pltpu.make_async_copy(ref, ref, first_send.at[n]).wait()
    for r in range(4):
        for d in (1, 2, 3):
            along_z(r, d).wait_send()
        if r:
            along_x(r).wait_send()
        for n in range(2):
            across(n, r).wait_send()
    whole = pl.ds(0, OWNERS - 1)
    pltpu.make_async_copy(send.at[whole], send.at[whole], send_sem).wait()
    pltpu.make_async_copy(recv.at[whole], recv.at[whole], recv_sem).wait()


def finish(
    owner, mode, recv, shadow, att_new_v, att_codes_v, att_amax_v,
    expert_new, expert_codes, expert_amax, attn_new, attn_codes, attn_amax,
    place, new_v, codes_v, amax_v, att_small, out_sem, new_sem, codes_sem,
):
    copy_an = pltpu.make_async_copy(att_new_v, attn_new, out_sem.at[0])
    copy_ac = pltpu.make_async_copy(att_codes_v, attn_codes, out_sem.at[1])

    def invert(l, _):
        place[owner[l]] = l
        return 0

    lax.fori_loop(0, OWNERS, invert, 0, unroll=8)

    def group_rows(s):
        return pl.ds(pl.multiple_of(s * (BLOCKS * RB), BLOCKS * RB), BLOCKS * RB)

    def copy_new(s):
        return pltpu.make_async_copy(new_v.at[group_rows(s)], expert_new.at[0, group_rows(s)], new_sem)

    def copy_codes(s):
        return pltpu.make_async_copy(codes_v.at[group_rows(s)], expert_codes.at[0, group_rows(s)], codes_sem)

    def group(s, _):
        for j in range(BLOCKS):
            rows = pl.ds(pl.multiple_of((s * BLOCKS + j) * RB, 8), RB)
            new_v[rows, :] = shadow[rows, :] + recv[place[s * BLOCKS + j]].astype(F32)
        copy_new(s).start()
        for j in range(TILES):
            i = s * TILES + j
            rows = pl.ds(pl.multiple_of(i * BLK, BLK), BLK)
            tile = new_v[rows, :]
            column = jnp.max(jnp.abs(tile), axis=0, keepdims=True)
            top = jnp.max(column, axis=1, keepdims=True)
            chosen = jnp.where(mode[i] == 0, jnp.broadcast_to(top, column.shape), column)
            amax_v[pl.ds(i, 1), :] = chosen
            codes_v[rows, :] = (tile * (1.0 / (chosen + 1e-6))).astype(BF16)
        copy_codes(s).start()
        return 0

    copy_an.start()
    copy_ac.start()
    lax.fori_loop(0, SUPER, group, 0)
    att_small[...] = att_amax_v[:, :ATT_TILES]
    copy_am = pltpu.make_async_copy(amax_v, expert_amax.at[0], out_sem.at[2])
    copy_am.start()
    copy_aa = pltpu.make_async_copy(att_small, attn_amax, out_sem.at[3])
    copy_aa.start()
    copy_an.wait()
    copy_ac.wait()
    copy_am.wait()
    copy_aa.wait()
    pltpu.make_async_copy(new_v, expert_new.at[0], new_sem).wait()
    pltpu.make_async_copy(codes_v, expert_codes.at[0], codes_sem).wait()


def on_device(learner_delta, owner_block, expert_shadow, tile_mode, attn_delta, attn_shadow):
    vmem = pl.BlockSpec(memory_space=pltpu.VMEM)
    hbm = pl.BlockSpec(memory_space=pltpu.HBM)
    smem = pl.BlockSpec(memory_space=pltpu.SMEM)
    dma = pltpu.SemaphoreType.DMA
    shape = jax.ShapeDtypeStruct
    in_hbm = functools.partial(pltpu.with_memory_space_constraint, memory_space=pltpu.HBM)
    recv, shadow, att_new_v, att_codes_v, att_amax_v = pl.pallas_call(
        exchange,
        name="exchange",
        out_shape=(
            pltpu.VMEM((OWNERS, RB, BLK), BF16),
            pltpu.VMEM((ROWS, BLK), F32),
            pltpu.VMEM((64, 8, ATT_COLS), F32),
            pltpu.VMEM((512, ATT_COLS), BF16),
            pltpu.VMEM((4, BLK), F32),
        ),
        in_specs=[hbm] * 4,
        out_specs=(vmem,) * 5,
        scratch_shapes=[
            pltpu.VMEM((RB, EXPERTS, 1024), BF16),
            pltpu.VMEM((SHARES, RB * EXPERTS, BLK), F32),
            pltpu.VMEM((OWNERS, RB, BLK), BF16),
            pltpu.VMEM((2, 4, 16, ATT_ROWS, WIDE_Z), BF16),
            pltpu.VMEM((2, 4, 16, ATT_ROWS, WIDE_X), BF16),
            pltpu.VMEM((16, ATT_ROWS, WIDE_Z), BF16),
            pltpu.VMEM((64, 8, ATT_COLS), F32),
            pltpu.VMEM((64, 8, ATT_COLS), F32),
            dma((6,)), dma(()), dma(()),
            dma((3,)), dma((3,)),
            dma((4, 4)), dma((4, 4)),
            dma((2, 4)), dma((2, 4)),
        ],
        compiler_params=pltpu.CompilerParams(
            collective_id=0, has_side_effects=True, vmem_limit_bytes=40 << 20
        ),
    )(*(in_hbm(x) for x in (learner_delta, attn_delta, attn_shadow.reshape(64, 8, ATT_COLS), expert_shadow)))

    return pl.pallas_call(
        finish,
        name="finish",
        out_shape=(
            shape((1, ROWS, BLK), F32),
            shape((1, ROWS, BLK), BF16),
            shape((1, ROWS // BLK, BLK), F32),
            shape((512, ATT_COLS), F32),
            shape((512, ATT_COLS), BF16),
            shape((4, ATT_TILES), F32),
        ),
        in_specs=[smem, smem] + [vmem] * 5,
        out_specs=(hbm,) * 6,
        scratch_shapes=[
            pltpu.SMEM((OWNERS,), jnp.int32),
            pltpu.VMEM((ROWS, BLK), F32),
            pltpu.VMEM((ROWS, BLK), BF16),
            pltpu.VMEM((ROWS // BLK, BLK), F32),
            pltpu.VMEM((4, ATT_TILES), F32),
            dma((4,)), dma(()), dma(()),
        ],
        compiler_params=pltpu.CompilerParams(vmem_limit_bytes=40 << 20),
    )(owner_block, tile_mode.reshape(ROWS // BLK), recv, shadow, att_new_v.reshape(512, ATT_COLS), att_codes_v, att_amax_v)


def solution(mesh):
    return jax.shard_map(
        on_device,
        mesh=mesh,
        in_specs=(
            P(("expert", "tensor"), None, None, None),
            P(),
            P("expert", None, "tensor"),
            P("expert", None, "tensor"),
            P(("expert", "tensor"), None),
            P(None, "tensor"),
        ),
        out_specs=(
            P("expert", None, "tensor"),
            P("expert", None, "tensor"),
            P("expert", None, "tensor"),
            P(None, "tensor"),
            P(None, "tensor"),
            P(None, "tensor"),
        ),
        check_vma=False,
    )
```

```python
import functools

import jax
import jax.numpy as jnp
from jax import lax
from jax.experimental import pallas as pl
from jax.experimental.pallas import tpu as pltpu
from jax.sharding import PartitionSpec as P

MESH = pl.DeviceIdType.MESH
BLK = 128
F32 = jnp.float32
BF16 = jnp.bfloat16

OWNERS = 128
RB = 56
EXPERTS = 16
SHARES = 8
ROWS = OWNERS * RB
ATT_ROWS = 4
ATT_COLS = 2048
ATT_TILES = ATT_COLS // BLK
SUPER = 8
BLOCKS = 16
TILES = 7


AHEAD, BETWEEN, UPTO = 50, 4, 90
STRIDE = 21


def exchange(
    delta, attn_delta, attn_shadow, expert_shadow,
    recv, shadow, attn_new, attn_codes, attn_amax,
    held, wide, send, gath, att_old, att_wide,
    load_sem, send_sem, recv_sem, first_send, first_recv, second_send, second_recv, third_send, third_recv,
    last_send, last_recv,
):
    e = lax.axis_index("expert")
    t = lax.axis_index("tensor")
    me = e * SHARES + t
    x, y, core = lax.div(e, 4), lax.rem(t, 4), lax.rem(e, 2)
    high, low = lax.div(t, 4), lax.rem(lax.div(e, 2), 2)
    z = high * 2 + low

    def step(v, d):
        return lax.rem(v + d, 4)

    def at(x, y, z, core):
        return x * 4 + lax.rem(z, 2) * 2 + core, lax.div(z, 2) * 4 + y

    load_delta = pltpu.make_async_copy(delta.at[0], held, load_sem.at[0])
    load_delta.start()

    barrier = pltpu.get_barrier_semaphore()
    for de in range(EXPERTS):
        for dt in range(SHARES):
            if de or dt:
                pl.semaphore_signal(
                    barrier, inc=1, device_id=(lax.rem(e + de, EXPERTS), lax.rem(t + dt, SHARES)), device_id_type=MESH
                )

    def columns(there, y):
        share = lax.div(there, 2) * 4 + y
        return attn_delta.at[:, pl.ds(pl.multiple_of(share * ATT_COLS, BLK), ATT_COLS)]

    mine = z * 4 + y
    own = pltpu.make_async_copy(columns(z, y), gath.at[core, x, mine], load_sem.at[1])
    own.start()
    load_att = pltpu.make_async_copy(attn_shadow, att_old, load_sem.at[2])
    load_att.start()
    load_exp = pltpu.make_async_copy(expert_shadow.at[0], shadow, load_sem.at[3])
    load_exp.start()

    load_delta.wait()

    def widen(r, _):
        rows = held[r].astype(F32)
        for j in range(SHARES):
            wide[j, pl.ds(pl.multiple_of(r * EXPERTS, EXPERTS), EXPERTS), :] = rows[:, j * BLK:(j + 1) * BLK]
        return 0

    lax.fori_loop(0, RB, widen, 0, unroll=2)

    def block_of(pe, pt):
        return wide[pt, pl.ds(pe, RB, stride=EXPERTS), :].astype(BF16)

    recv[me] = block_of(e, t)

    pl.semaphore_wait(barrier, OWNERS - 1)

    for k in (10, 5, 15, 7, 13, 2, 8, 9, 6, 11, 14, 1, 4, 3, 12):
        there, over = step(z, k // 4), step(y, k % 4)
        pltpu.make_async_remote_copy(
            src_ref=columns(there, over), dst_ref=gath.at[core, x, mine], send_sem=first_send, recv_sem=first_recv,
            device_id=at(x, over, there, core), device_id_type=MESH,
        ).start()

    def send_block(k, _):
        s = lax.rem(k * STRIDE, 32)
        dx = jnp.where(k <= 32, 2, jnp.where(k <= 64, 1, jnp.where(k <= 96, 3, 0)))
        dy, dz = lax.div(s, 8), lax.rem(lax.div(s, 2), 4)
        pe, pt = at(step(x, dx), step(y, dy), step(z, dz), lax.rem(core + s, 2))
        p = pe * SHARES + pt
        send[p] = block_of(pe, pt)
        pltpu.make_async_remote_copy(
            src_ref=send.at[p],
            dst_ref=recv.at[me],
            send_sem=send_sem,
            recv_sem=recv_sem,
            device_id=(pe, pt),
            device_id_type=MESH,
        ).start()
        return 0

    lax.fori_loop(1, AHEAD, send_block, 0)

    own.wait()
    landed = gath.at[0, 0, pl.ds(0, 15)]
    pltpu.make_async_copy(landed, landed, first_recv).wait()

    sides = (1, 3)

    def half(h):
        return pl.ds(8 * h, 8)

    def hand(i, rows, to, sent, got):
        ref = gath.at[core, i, rows]
        return pltpu.make_async_remote_copy(
            src_ref=ref, dst_ref=ref, send_sem=sent, recv_sem=got, device_id=to, device_id_type=MESH
        )

    def beside(n, h):
        return hand(x, half(h), at(step(x, sides[n]), y, z, core), second_send.at[n, h], second_recv.at[n, h])

    def onward(n):
        return hand(
            step(x, 4 - sides[n]), half(n), at(step(x, sides[n]), y, z, core), third_send.at[n], third_recv.at[n]
        )

    def across(n):
        i, rows = ((0, pl.ds(0, 16)), (3, pl.ds(0, 16)), (1, pl.ds(0, 16)), (2, half(0)), (2, half(1)))[n]
        return hand(step(x, i), rows, at(x, y, z, 1 - core), last_send.at[n], last_recv.at[n])

    k = AHEAD
    for start in (
        beside(0, 0).start, beside(1, 1).start, beside(0, 1).start, beside(1, 0).start, across(0).start
    ):
        start()
        lax.fori_loop(k, k + BETWEEN, send_block, 0)
        k += BETWEEN
    lax.fori_loop(k, UPTO, send_block, 0)
    for n in range(2):
        beside(n, n).wait_recv()
        onward(n).start()
    lax.fori_loop(UPTO, OWNERS, send_block, 0)

    def att_widen(m, _):
        i, j = lax.div(m, 4), lax.rem(m, 4)
        gx, gc = lax.div(i, 4), lax.rem(i, 2)
        gz = lax.div(j, 2) * 2 + lax.rem(lax.div(i, 2), 2)
        for n in range(2):
            owner = gz * 4 + lax.rem(j, 2) * 2 + n
            rows = slice(4 * n, 4 * n + 4)
            att_wide[m, rows, :] = gath[gc, gx, owner].astype(F32)
        return 0

    def att_tile_row(i, _):
        tops = []
        for j in range(ATT_TILES):
            cols = slice(j * BLK, (j + 1) * BLK)
            groups = pl.ds(i * 16, 16)
            new = att_old[groups, :, cols] + att_wide[groups, :, cols]
            attn_new[groups, :, cols] = new
            top = jnp.max(jnp.max(jnp.max(jnp.abs(new), axis=0), axis=0, keepdims=True), axis=1, keepdims=True)
            codes = new * (1.0 / (top + 1e-6))[None]
            attn_codes[pl.ds(pl.multiple_of(i * BLK, BLK), BLK), cols] = codes.reshape(BLK, BLK).astype(BF16)
            tops.append(jnp.broadcast_to(top, (1, BLK)))
        lane = lax.broadcasted_iota(jnp.int32, (1, BLK), 1)
        row = jnp.zeros((1, BLK), F32)
        for j in range(ATT_TILES):
            row = jnp.where(lane == j, tops[j], row)
        attn_amax[pl.ds(i, 1), :] = row
        return 0

    load_att.wait()

    def work(r):
        i = step(x, r)
        lax.fori_loop(i * 16, i * 16 + 16, att_widen, 0)
        att_tile_row(i, 0)

    across(0).wait_recv()
    work(0)
    for n in range(2):
        beside(n, 1 - n).wait_recv()
        across(1 + n).start()
    for n in range(2):
        across(1 + n).wait_recv()
        work((3, 1)[n])
    for n in range(2):
        onward(n).wait_recv()
        across(3 + n).start()
    for n in range(2):
        across(3 + n).wait_recv()
    work(2)

    load_exp.wait()
    pltpu.make_async_copy(landed, landed, first_send).wait()
    for n in range(2):
        beside(n, 0).wait_send()
        beside(n, 1).wait_send()
        onward(n).wait_send()
    for n in range(5):
        across(n).wait_send()
    whole = pl.ds(0, OWNERS - 1)
    pltpu.make_async_copy(send.at[whole], send.at[whole], send_sem).wait()
    pltpu.make_async_copy(recv.at[whole], recv.at[whole], recv_sem).wait()


def finish(
    owner, mode, recv, shadow, att_new_v, att_codes_v, att_amax_v,
    expert_new, expert_codes, expert_amax, attn_new, attn_codes, attn_amax,
    place, new_v, codes_v, amax_v, att_small, out_sem, new_sem, codes_sem,
):
    copy_an = pltpu.make_async_copy(att_new_v, attn_new, out_sem.at[0])
    copy_ac = pltpu.make_async_copy(att_codes_v, attn_codes, out_sem.at[1])

    copy_an.start()
    copy_ac.start()

    def invert(l, _):
        place[owner[l]] = l
        return 0

    lax.fori_loop(0, OWNERS, invert, 0, unroll=8)

    def group_rows(s):
        return pl.ds(pl.multiple_of(s * (BLOCKS * RB), BLOCKS * RB), BLOCKS * RB)

    def copy_new(s):
        return pltpu.make_async_copy(new_v.at[group_rows(s)], expert_new.at[0, group_rows(s)], new_sem)

    def copy_codes(s):
        return pltpu.make_async_copy(codes_v.at[group_rows(s)], expert_codes.at[0, group_rows(s)], codes_sem)

    def group(s, _):
        for j in range(BLOCKS):
            rows = pl.ds(pl.multiple_of((s * BLOCKS + j) * RB, 8), RB)
            new_v[rows, :] = shadow[rows, :] + recv[place[s * BLOCKS + j]].astype(F32)
        copy_new(s).start()
        for j in range(TILES):
            i = s * TILES + j
            rows = pl.ds(pl.multiple_of(i * BLK, BLK), BLK)
            tile = new_v[rows, :]
            column = jnp.max(jnp.abs(tile), axis=0, keepdims=True)
            top = jnp.max(column, axis=1, keepdims=True)
            chosen = jnp.where(mode[i] == 0, jnp.broadcast_to(top, column.shape), column)
            amax_v[pl.ds(i, 1), :] = chosen
            codes_v[rows, :] = (tile * (1.0 / (chosen + 1e-6))).astype(BF16)
        copy_codes(s).start()
        return 0

    lax.fori_loop(0, SUPER, group, 0)
    att_small[...] = att_amax_v[:, :ATT_TILES]
    copy_am = pltpu.make_async_copy(amax_v, expert_amax.at[0], out_sem.at[2])
    copy_am.start()
    copy_aa = pltpu.make_async_copy(att_small, attn_amax, out_sem.at[3])
    copy_aa.start()
    copy_an.wait()
    copy_ac.wait()
    copy_am.wait()
    copy_aa.wait()
    pltpu.make_async_copy(new_v, expert_new.at[0], new_sem).wait()
    pltpu.make_async_copy(codes_v, expert_codes.at[0], codes_sem).wait()


def on_device(learner_delta, owner_block, expert_shadow, tile_mode, attn_delta, attn_shadow):
    vmem = pl.BlockSpec(memory_space=pltpu.VMEM)
    hbm = pl.BlockSpec(memory_space=pltpu.HBM)
    smem = pl.BlockSpec(memory_space=pltpu.SMEM)
    dma = pltpu.SemaphoreType.DMA
    shape = jax.ShapeDtypeStruct
    in_hbm = functools.partial(pltpu.with_memory_space_constraint, memory_space=pltpu.HBM)
    recv, shadow, att_new_v, att_codes_v, att_amax_v = pl.pallas_call(
        exchange,
        name="exchange",
        out_shape=(
            pltpu.VMEM((OWNERS, RB, BLK), BF16),
            pltpu.VMEM((ROWS, BLK), F32),
            pltpu.VMEM((64, 8, ATT_COLS), F32),
            pltpu.VMEM((512, ATT_COLS), BF16),
            pltpu.VMEM((4, BLK), F32),
        ),
        in_specs=[hbm] * 4,
        out_specs=(vmem,) * 5,
        scratch_shapes=[
            pltpu.VMEM((RB, EXPERTS, 1024), BF16),
            pltpu.VMEM((SHARES, RB * EXPERTS, BLK), F32),
            pltpu.VMEM((OWNERS, RB, BLK), BF16),
            pltpu.VMEM((2, 4, 16, ATT_ROWS, ATT_COLS), BF16),
            pltpu.VMEM((64, 8, ATT_COLS), F32),
            pltpu.VMEM((64, 8, ATT_COLS), F32),
            dma((4,)), dma(()), dma(()), dma(()), dma(()),
            dma((2, 2)), dma((2, 2)), dma((2,)), dma((2,)), dma((5,)), dma((5,)),
        ],
        compiler_params=pltpu.CompilerParams(
            collective_id=0, has_side_effects=True, vmem_limit_bytes=40 << 20
        ),
    )(*(in_hbm(x) for x in (learner_delta, attn_delta, attn_shadow.reshape(64, 8, ATT_COLS), expert_shadow)))

    return pl.pallas_call(
        finish,
        name="finish",
        out_shape=(
            shape((1, ROWS, BLK), F32),
            shape((1, ROWS, BLK), BF16),
            shape((1, ROWS // BLK, BLK), F32),
            shape((512, ATT_COLS), F32),
            shape((512, ATT_COLS), BF16),
            shape((4, ATT_TILES), F32),
        ),
        in_specs=[smem, smem] + [vmem] * 5,
        out_specs=(hbm,) * 6,
        scratch_shapes=[
            pltpu.SMEM((OWNERS,), jnp.int32),
            pltpu.VMEM((ROWS, BLK), F32),
            pltpu.VMEM((ROWS, BLK), BF16),
            pltpu.VMEM((ROWS // BLK, BLK), F32),
            pltpu.VMEM((4, ATT_TILES), F32),
            dma((4,)), dma(()), dma(()),
        ],
        compiler_params=pltpu.CompilerParams(vmem_limit_bytes=40 << 20),
    )(owner_block, tile_mode.reshape(ROWS // BLK), recv, shadow, att_new_v.reshape(512, ATT_COLS), att_codes_v, att_amax_v)


def solution(mesh):
    return jax.shard_map(
        on_device,
        mesh=mesh,
        in_specs=(
            P(("expert", "tensor"), None, None, None),
            P(),
            P("expert", None, "tensor"),
            P("expert", None, "tensor"),
            P(("expert", "tensor"), None),
            P(None, "tensor"),
        ),
        out_specs=(
            P("expert", None, "tensor"),
            P("expert", None, "tensor"),
            P("expert", None, "tensor"),
            P(None, "tensor"),
            P(None, "tensor"),
            P(None, "tensor"),
        ),
        check_vma=False,
    )
```

```python
import functools

import jax
import jax.numpy as jnp
from jax import lax
from jax.experimental import pallas as pl
from jax.experimental.pallas import tpu as pltpu
from jax.sharding import PartitionSpec as P

MESH = pl.DeviceIdType.MESH
BLK = 128
F32 = jnp.float32
BF16 = jnp.bfloat16

OWNERS = 128
RB = 56
EXPERTS = 16
SHARES = 8
ROWS = OWNERS * RB
ATT_ROWS = 4
ATT_COLS = 2048
ATT_TILES = ATT_COLS // BLK
SUPER = 8
BLOCKS = 16
TILES = 7


AHEAD, BETWEEN, UPTO = 65, 4, 127
STRIDE = 21


def exchange(
    delta, attn_delta, attn_shadow, expert_shadow,
    recv, shadow, attn_new, attn_codes, attn_amax,
    held, wide, send, gath, att_old, att_wide,
    load_sem, send_sem, recv_sem, first_send, first_recv, second_send, second_recv, third_send, third_recv,
    last_send, last_recv,
):
    e = lax.axis_index("expert")
    t = lax.axis_index("tensor")
    me = e * SHARES + t
    x, y, core = lax.div(e, 4), lax.rem(t, 4), lax.rem(e, 2)
    high, low = lax.div(t, 4), lax.rem(lax.div(e, 2), 2)
    z = high * 2 + low

    def step(v, d):
        return lax.rem(v + d, 4)

    def at(x, y, z, core):
        return x * 4 + lax.rem(z, 2) * 2 + core, lax.div(z, 2) * 4 + y

    load_delta = pltpu.make_async_copy(delta.at[0], held, load_sem.at[0])
    load_delta.start()

    barrier = pltpu.get_barrier_semaphore()
    for de in range(EXPERTS):
        for dt in range(SHARES):
            if de or dt:
                pl.semaphore_signal(
                    barrier, inc=1, device_id=(lax.rem(e + de, EXPERTS), lax.rem(t + dt, SHARES)), device_id_type=MESH
                )

    def columns(there, y):
        share = lax.div(there, 2) * 4 + y
        return attn_delta.at[:, pl.ds(pl.multiple_of(share * ATT_COLS, BLK), ATT_COLS)]

    mine = z * 4 + y
    own = pltpu.make_async_copy(columns(z, y), gath.at[core, x, mine], load_sem.at[1])
    own.start()
    load_att = pltpu.make_async_copy(attn_shadow, att_old, load_sem.at[2])
    load_att.start()
    load_exp = pltpu.make_async_copy(expert_shadow.at[0], shadow, load_sem.at[3])
    load_exp.start()

    load_delta.wait()

    def widen(r, _):
        rows = held[r].astype(F32)
        for j in range(SHARES):
            wide[j, pl.ds(pl.multiple_of(r * EXPERTS, EXPERTS), EXPERTS), :] = rows[:, j * BLK:(j + 1) * BLK]
        return 0

    lax.fori_loop(0, RB, widen, 0, unroll=2)

    def block_of(pe, pt):
        return wide[pt, pl.ds(pe, RB, stride=EXPERTS), :].astype(BF16)

    recv[me] = block_of(e, t)

    pl.semaphore_wait(barrier, OWNERS - 1)

    for k in (10, 5, 15, 7, 13, 2, 8, 9, 6, 11, 14, 1, 4, 3, 12):
        there, over = step(z, k // 4), step(y, k % 4)
        pltpu.make_async_remote_copy(
            src_ref=columns(there, over), dst_ref=gath.at[core, x, mine], send_sem=first_send, recv_sem=first_recv,
            device_id=at(x, over, there, core), device_id_type=MESH,
        ).start()

    def send_block(k, _):
        n = k - 1
        s = lax.rem((n + 1) * STRIDE, 32)
        dx = jnp.where(n < 32, 2, jnp.where(n < 64, 1, jnp.where(n < 96, 3, 0)))
        dy, dz = lax.div(s, 8), lax.rem(lax.div(s, 2), 4)
        pe, pt = at(step(x, dx), step(y, dy), step(z, dz), lax.rem(core + s, 2))
        p = pe * SHARES + pt
        send[p] = block_of(pe, pt)
        pltpu.make_async_remote_copy(
            src_ref=send.at[p],
            dst_ref=recv.at[me],
            send_sem=send_sem,
            recv_sem=recv_sem,
            device_id=(pe, pt),
            device_id_type=MESH,
        ).start()
        return 0

    lax.fori_loop(1, AHEAD, send_block, 0)

    own.wait()
    landed = gath.at[0, 0, pl.ds(0, 15)]
    pltpu.make_async_copy(landed, landed, first_recv).wait()

    sides = (1, 3)

    def half(h):
        return pl.ds(8 * h, 8)

    def hand(i, rows, to, sent, got):
        ref = gath.at[core, i, rows]
        return pltpu.make_async_remote_copy(
            src_ref=ref, dst_ref=ref, send_sem=sent, recv_sem=got, device_id=to, device_id_type=MESH
        )

    def beside(n, h):
        return hand(x, half(h), at(step(x, sides[n]), y, z, core), second_send.at[n, h], second_recv.at[n, h])

    def onward(n):
        return hand(
            step(x, 4 - sides[n]), half(n), at(step(x, sides[n]), y, z, core), third_send.at[n], third_recv.at[n]
        )

    def across(n):
        i, rows = ((0, pl.ds(0, 16)), (3, pl.ds(0, 16)), (1, pl.ds(0, 16)), (2, half(0)), (2, half(1)))[n]
        return hand(step(x, i), rows, at(x, y, z, 1 - core), last_send.at[n], last_recv.at[n])

    k = AHEAD
    for start in (
        beside(0, 0).start, beside(1, 1).start, beside(0, 1).start, beside(1, 0).start, across(0).start
    ):
        start()
        lax.fori_loop(k, k + BETWEEN, send_block, 0)
        k += BETWEEN
    lax.fori_loop(k, UPTO, send_block, 0)
    for n in range(2):
        beside(n, n).wait_recv()
        onward(n).start()
    lax.fori_loop(UPTO, OWNERS, send_block, 0)

    def att_widen(m, _):
        i, j = lax.div(m, 4), lax.rem(m, 4)
        gx, gc = lax.div(i, 4), lax.rem(i, 2)
        gz = lax.div(j, 2) * 2 + lax.rem(lax.div(i, 2), 2)
        for n in range(2):
            owner = gz * 4 + lax.rem(j, 2) * 2 + n
            rows = slice(4 * n, 4 * n + 4)
            att_wide[m, rows, :] = gath[gc, gx, owner].astype(F32)
        return 0

    def att_tile_row(i, _):
        tops = []
        for j in range(ATT_TILES):
            cols = slice(j * BLK, (j + 1) * BLK)
            groups = pl.ds(i * 16, 16)
            new = att_old[groups, :, cols] + att_wide[groups, :, cols]
            attn_new[groups, :, cols] = new
            top = jnp.max(jnp.max(jnp.max(jnp.abs(new), axis=0), axis=0, keepdims=True), axis=1, keepdims=True)
            codes = new * (1.0 / (top + 1e-6))[None]
            attn_codes[pl.ds(pl.multiple_of(i * BLK, BLK), BLK), cols] = codes.reshape(BLK, BLK).astype(BF16)
            tops.append(jnp.broadcast_to(top, (1, BLK)))
        lane = lax.broadcasted_iota(jnp.int32, (1, BLK), 1)
        row = jnp.zeros((1, BLK), F32)
        for j in range(ATT_TILES):
            row = jnp.where(lane == j, tops[j], row)
        attn_amax[pl.ds(i, 1), :] = row
        return 0

    load_att.wait()

    def work(r):
        i = step(x, r)
        lax.fori_loop(i * 16, i * 16 + 16, att_widen, 0)
        att_tile_row(i, 0)

    across(0).wait_recv()
    work(0)
    for n in range(2):
        beside(n, 1 - n).wait_recv()
        across(1 + n).start()
    for n in range(2):
        across(1 + n).wait_recv()
        work((3, 1)[n])
    for n in range(2):
        onward(n).wait_recv()
        across(3 + n).start()
    for n in range(2):
        across(3 + n).wait_recv()
    work(2)

    load_exp.wait()
    pltpu.make_async_copy(landed, landed, first_send).wait()
    for n in range(2):
        beside(n, 0).wait_send()
        beside(n, 1).wait_send()
        onward(n).wait_send()
    for n in range(5):
        across(n).wait_send()
    whole = pl.ds(0, OWNERS - 1)
    pltpu.make_async_copy(send.at[whole], send.at[whole], send_sem).wait()
    pltpu.make_async_copy(recv.at[whole], recv.at[whole], recv_sem).wait()


def finish(
    owner_v, mode_v, recv, shadow, att_new_v, att_codes_v, att_amax_v,
    expert_new, expert_codes, expert_amax, attn_new, attn_codes, attn_amax,
    owner, mode, place, new_v, codes_v, amax_v, att_small, out_sem, new_sem, codes_sem,
):
    copy_an = pltpu.make_async_copy(att_new_v, attn_new, out_sem.at[0])
    copy_ac = pltpu.make_async_copy(att_codes_v, attn_codes, out_sem.at[1])

    copy_owner = pltpu.make_async_copy(owner_v, owner, out_sem.at[4])
    copy_mode = pltpu.make_async_copy(mode_v, mode, out_sem.at[5])
    copy_owner.start()
    copy_mode.start()
    copy_an.start()
    copy_ac.start()
    att_small[...] = att_amax_v[:, :ATT_TILES]
    copy_aa = pltpu.make_async_copy(att_small, attn_amax, out_sem.at[3])
    copy_aa.start()
    copy_owner.wait()
    copy_mode.wait()

    def invert(l, _):
        place[owner[l]] = l
        return 0

    lax.fori_loop(0, OWNERS, invert, 0, unroll=8)

    def group_rows(s):
        return pl.ds(pl.multiple_of(s * (BLOCKS * RB), BLOCKS * RB), BLOCKS * RB)

    def copy_new(s):
        return pltpu.make_async_copy(new_v.at[group_rows(s)], expert_new.at[0, group_rows(s)], new_sem)

    def copy_codes(s):
        return pltpu.make_async_copy(codes_v.at[group_rows(s)], expert_codes.at[0, group_rows(s)], codes_sem)

    def group(s, _):
        for j in range(BLOCKS):
            rows = pl.ds(pl.multiple_of((s * BLOCKS + j) * RB, 8), RB)
            new_v[rows, :] = shadow[rows, :] + recv[place[s * BLOCKS + j]].astype(F32)
        copy_new(s).start()
        for j in range(TILES):
            i = s * TILES + j
            rows = pl.ds(pl.multiple_of(i * BLK, BLK), BLK)
            tile = new_v[rows, :]
            column = jnp.max(jnp.abs(tile), axis=0, keepdims=True)
            top = jnp.max(column, axis=1, keepdims=True)
            chosen = jnp.where(mode[i] == 0, jnp.broadcast_to(top, column.shape), column)
            amax_v[pl.ds(i, 1), :] = chosen
            codes_v[rows, :] = (tile * (1.0 / (chosen + 1e-6))).astype(BF16)
        copy_codes(s).start()
        return 0

    lax.fori_loop(0, SUPER, group, 0)
    copy_am = pltpu.make_async_copy(amax_v, expert_amax.at[0], out_sem.at[2])
    copy_am.start()
    copy_an.wait()
    copy_ac.wait()
    copy_am.wait()
    copy_aa.wait()
    pltpu.make_async_copy(new_v, expert_new.at[0], new_sem).wait()
    pltpu.make_async_copy(codes_v, expert_codes.at[0], codes_sem).wait()


def on_device(learner_delta, owner_block, expert_shadow, tile_mode, attn_delta, attn_shadow):
    vmem = pl.BlockSpec(memory_space=pltpu.VMEM)
    hbm = pl.BlockSpec(memory_space=pltpu.HBM)
    dma = pltpu.SemaphoreType.DMA
    shape = jax.ShapeDtypeStruct
    in_hbm = functools.partial(pltpu.with_memory_space_constraint, memory_space=pltpu.HBM)
    recv, shadow, att_new_v, att_codes_v, att_amax_v = pl.pallas_call(
        exchange,
        name="exchange",
        out_shape=(
            pltpu.VMEM((OWNERS, RB, BLK), BF16),
            pltpu.VMEM((ROWS, BLK), F32),
            pltpu.VMEM((64, 8, ATT_COLS), F32),
            pltpu.VMEM((512, ATT_COLS), BF16),
            pltpu.VMEM((4, BLK), F32),
        ),
        in_specs=[hbm] * 4,
        out_specs=(vmem,) * 5,
        scratch_shapes=[
            pltpu.VMEM((RB, EXPERTS, 1024), BF16),
            pltpu.VMEM((SHARES, RB * EXPERTS, BLK), F32),
            pltpu.VMEM((OWNERS, RB, BLK), BF16),
            pltpu.VMEM((2, 4, 16, ATT_ROWS, ATT_COLS), BF16),
            pltpu.VMEM((64, 8, ATT_COLS), F32),
            pltpu.VMEM((64, 8, ATT_COLS), F32),
            dma((4,)), dma(()), dma(()), dma(()), dma(()),
            dma((2, 2)), dma((2, 2)), dma((2,)), dma((2,)), dma((5,)), dma((5,)),
        ],
        compiler_params=pltpu.CompilerParams(
            collective_id=0, has_side_effects=True, vmem_limit_bytes=40 << 20
        ),
    )(*(in_hbm(x) for x in (learner_delta, attn_delta, attn_shadow.reshape(64, 8, ATT_COLS), expert_shadow)))

    return pl.pallas_call(
        finish,
        name="finish",
        out_shape=(
            shape((1, ROWS, BLK), F32),
            shape((1, ROWS, BLK), BF16),
            shape((1, ROWS // BLK, BLK), F32),
            shape((512, ATT_COLS), F32),
            shape((512, ATT_COLS), BF16),
            shape((4, ATT_TILES), F32),
        ),
        in_specs=[vmem] * 7,
        out_specs=(hbm,) * 6,
        scratch_shapes=[
            pltpu.SMEM((OWNERS,), jnp.int32),
            pltpu.SMEM((ROWS // BLK,), jnp.int32),
            pltpu.SMEM((OWNERS,), jnp.int32),
            pltpu.VMEM((ROWS, BLK), F32),
            pltpu.VMEM((ROWS, BLK), BF16),
            pltpu.VMEM((ROWS // BLK, BLK), F32),
            pltpu.VMEM((4, ATT_TILES), F32),
            dma((6,)), dma(()), dma(()),
        ],
        compiler_params=pltpu.CompilerParams(vmem_limit_bytes=40 << 20),
    )(owner_block, tile_mode.reshape(ROWS // BLK), recv, shadow, att_new_v.reshape(512, ATT_COLS), att_codes_v, att_amax_v)


def solution(mesh):
    return jax.shard_map(
        on_device,
        mesh=mesh,
        in_specs=(
            P(("expert", "tensor"), None, None, None),
            P(),
            P("expert", None, "tensor"),
            P("expert", None, "tensor"),
            P(("expert", "tensor"), None),
            P(None, "tensor"),
        ),
        out_specs=(
            P("expert", None, "tensor"),
            P("expert", None, "tensor"),
            P("expert", None, "tensor"),
            P(None, "tensor"),
            P(None, "tensor"),
            P(None, "tensor"),
        ),
        check_vma=False,
    )
```

```python
import functools

import jax
import jax.numpy as jnp
from jax import lax
from jax.experimental import pallas as pl
from jax.experimental.pallas import tpu as pltpu
from jax.sharding import PartitionSpec as P

MESH = pl.DeviceIdType.MESH
BLK = 128
F32 = jnp.float32
BF16 = jnp.bfloat16

OWNERS = 128
RB = 56
EXPERTS = 16
SHARES = 8
ROWS = OWNERS * RB
ATT_ROWS = 4
ATT_COLS = 2048
ATT_TILES = ATT_COLS // BLK
SUPER = 8
BLOCKS = 16
TILES = 7


AHEAD, BETWEEN, UPTO = 65, 4, 127
STRIDE = 21


def exchange(
    delta, attn_delta, attn_shadow, expert_shadow,
    recv, shadow, attn_new, attn_codes, attn_amax,
    held, wide, send, gath, att_old, att_wide,
    load_sem, send_sem, recv_sem, first_send, first_recv, second_send, second_recv, third_send, third_recv,
    last_send, last_recv,
):
    e = lax.axis_index("expert")
    t = lax.axis_index("tensor")
    me = e * SHARES + t
    x, y, core = lax.div(e, 4), lax.rem(t, 4), lax.rem(e, 2)
    high, low = lax.div(t, 4), lax.rem(lax.div(e, 2), 2)
    z = high * 2 + low

    def step(v, d):
        return lax.rem(v + d, 4)

    def at(x, y, z, core):
        return x * 4 + lax.rem(z, 2) * 2 + core, lax.div(z, 2) * 4 + y

    load_delta = pltpu.make_async_copy(delta.at[0], held, load_sem.at[0])
    load_delta.start()

    to_x = [step(x, d) * 4 for d in range(4)]
    to_y = [step(y, d) for d in range(4)]
    to_z = [(lax.rem(step(z, d), 2) * 2, lax.div(step(z, d), 2) * 4) for d in range(4)]
    to_core = (core, 1 - core)
    barrier = pltpu.get_barrier_semaphore()
    for s in sorted(range(1, OWNERS), key=lambda s: -sum(min(d, 4 - d) for d in (s // 32, s // 8 % 4, s // 2 % 4))):
        near, far = to_z[s // 2 % 4]
        pl.semaphore_signal(
            barrier, inc=1, device_id=(to_x[s // 32] + near + to_core[s % 2], far + to_y[s // 8 % 4]), device_id_type=MESH
        )

    def columns(there, y):
        share = lax.div(there, 2) * 4 + y
        return attn_delta.at[:, pl.ds(pl.multiple_of(share * ATT_COLS, BLK), ATT_COLS)]

    mine = z * 4 + y
    own = pltpu.make_async_copy(columns(z, y), gath.at[core, x, mine], load_sem.at[1])
    own.start()
    load_att = pltpu.make_async_copy(attn_shadow, att_old, load_sem.at[2])
    load_att.start()
    load_exp = pltpu.make_async_copy(expert_shadow.at[0], shadow, load_sem.at[3])
    load_exp.start()

    load_delta.wait()

    def widen(r, _):
        rows = held[r].astype(F32)
        for j in range(SHARES):
            wide[j, pl.ds(pl.multiple_of(r * EXPERTS, EXPERTS), EXPERTS), :] = rows[:, j * BLK:(j + 1) * BLK]
        return 0

    lax.fori_loop(0, RB, widen, 0, unroll=2)

    def block_of(pe, pt):
        return wide[pt, pl.ds(pe, RB, stride=EXPERTS), :].astype(BF16)

    recv[me] = block_of(e, t)

    pl.semaphore_wait(barrier, OWNERS - 1)

    for k in (10, 5, 15, 7, 13, 2, 8, 9, 6, 11, 14, 1, 4, 3, 12):
        there, over = step(z, k // 4), step(y, k % 4)
        pltpu.make_async_remote_copy(
            src_ref=columns(there, over), dst_ref=gath.at[core, x, mine], send_sem=first_send, recv_sem=first_recv,
            device_id=at(x, over, there, core), device_id_type=MESH,
        ).start()

    def send_block(k, _):
        s = lax.rem(k * STRIDE, 32)
        dx = jnp.where(k <= 32, 2, jnp.where(k <= 64, 1, jnp.where(k <= 96, 3, 0)))
        dy, dz = lax.div(s, 8), lax.rem(lax.div(s, 2), 4)
        pe, pt = at(step(x, dx), step(y, dy), step(z, dz), lax.rem(core + s, 2))
        p = pe * SHARES + pt
        send[p] = block_of(pe, pt)
        pltpu.make_async_remote_copy(
            src_ref=send.at[p],
            dst_ref=recv.at[me],
            send_sem=send_sem,
            recv_sem=recv_sem,
            device_id=(pe, pt),
            device_id_type=MESH,
        ).start()
        return 0

    lax.fori_loop(1, AHEAD, send_block, 0)

    own.wait()
    landed = gath.at[0, 0, pl.ds(0, 15)]
    pltpu.make_async_copy(landed, landed, first_recv).wait()

    sides = (1, 3)

    def half(h):
        return pl.ds(8 * h, 8)

    def hand(i, rows, to, sent, got):
        ref = gath.at[core, i, rows]
        return pltpu.make_async_remote_copy(
            src_ref=ref, dst_ref=ref, send_sem=sent, recv_sem=got, device_id=to, device_id_type=MESH
        )

    def beside(n, h):
        return hand(x, half(h), at(step(x, sides[n]), y, z, core), second_send.at[n, h], second_recv.at[n, h])

    def onward(n):
        return hand(
            step(x, 4 - sides[n]), half(n), at(step(x, sides[n]), y, z, core), third_send.at[n], third_recv.at[n]
        )

    def across(n):
        i, rows = ((0, pl.ds(0, 16)), (3, pl.ds(0, 16)), (1, pl.ds(0, 16)), (2, half(0)), (2, half(1)))[n]
        return hand(step(x, i), rows, at(x, y, z, 1 - core), last_send.at[n], last_recv.at[n])

    k = AHEAD
    for start in (
        beside(0, 0).start, beside(1, 1).start, beside(0, 1).start, beside(1, 0).start, across(0).start
    ):
        start()
        lax.fori_loop(k, k + BETWEEN, send_block, 0)
        k += BETWEEN
    lax.fori_loop(k, UPTO, send_block, 0)
    for n in range(2):
        beside(n, n).wait_recv()
        onward(n).start()
    lax.fori_loop(UPTO, OWNERS, send_block, 0)

    def att_widen(m, _):
        i, j = lax.div(m, 4), lax.rem(m, 4)
        gx, gc = lax.div(i, 4), lax.rem(i, 2)
        gz = lax.div(j, 2) * 2 + lax.rem(lax.div(i, 2), 2)
        for n in range(2):
            owner = gz * 4 + lax.rem(j, 2) * 2 + n
            rows = slice(4 * n, 4 * n + 4)
            att_wide[m, rows, :] = gath[gc, gx, owner].astype(F32)
        return 0

    def att_tile_row(i, _):
        tops = []
        for j in range(ATT_TILES):
            cols = slice(j * BLK, (j + 1) * BLK)
            groups = pl.ds(i * 16, 16)
            new = att_old[groups, :, cols] + att_wide[groups, :, cols]
            attn_new[groups, :, cols] = new
            top = jnp.max(jnp.max(jnp.max(jnp.abs(new), axis=0), axis=0, keepdims=True), axis=1, keepdims=True)
            codes = new * (1.0 / (top + 1e-6))[None]
            attn_codes[pl.ds(pl.multiple_of(i * BLK, BLK), BLK), cols] = codes.reshape(BLK, BLK).astype(BF16)
            tops.append(jnp.broadcast_to(top, (1, BLK)))
        lane = lax.broadcasted_iota(jnp.int32, (1, BLK), 1)
        row = jnp.zeros((1, BLK), F32)
        for j in range(ATT_TILES):
            row = jnp.where(lane == j, tops[j], row)
        attn_amax[pl.ds(i, 1), :] = row
        return 0

    load_att.wait()

    def work(r):
        i = step(x, r)
        lax.fori_loop(i * 16, i * 16 + 16, att_widen, 0)
        att_tile_row(i, 0)

    across(0).wait_recv()
    work(0)
    for n in range(2):
        beside(n, 1 - n).wait_recv()
        across(1 + n).start()
    for n in range(2):
        across(1 + n).wait_recv()
        work((3, 1)[n])
    for n in range(2):
        onward(n).wait_recv()
        across(3 + n).start()
    for n in range(2):
        across(3 + n).wait_recv()
    work(2)

    load_exp.wait()
    pltpu.make_async_copy(landed, landed, first_send).wait()
    for n in range(2):
        beside(n, 0).wait_send()
        beside(n, 1).wait_send()
        onward(n).wait_send()
    for n in range(5):
        across(n).wait_send()
    whole = pl.ds(0, OWNERS - 1)
    pltpu.make_async_copy(send.at[whole], send.at[whole], send_sem).wait()
    pltpu.make_async_copy(recv.at[whole], recv.at[whole], recv_sem).wait()


def finish(
    owner_v, mode_v, recv, shadow, att_new_v, att_codes_v, att_amax_v,
    expert_new, expert_codes, expert_amax, attn_new, attn_codes, attn_amax,
    owner, mode, place, new_v, codes_v, amax_v, att_small, out_sem, new_sem, codes_sem,
):
    copy_an = pltpu.make_async_copy(att_new_v, attn_new, out_sem.at[0])
    copy_ac = pltpu.make_async_copy(att_codes_v, attn_codes, out_sem.at[1])

    copy_owner = pltpu.make_async_copy(owner_v, owner, out_sem.at[4])
    copy_mode = pltpu.make_async_copy(mode_v, mode, out_sem.at[5])
    copy_owner.start()
    copy_mode.start()
    copy_an.start()
    copy_ac.start()
    att_small[...] = att_amax_v[:, :ATT_TILES]
    copy_aa = pltpu.make_async_copy(att_small, attn_amax, out_sem.at[3])
    copy_aa.start()
    copy_owner.wait()
    copy_mode.wait()

    def invert(l, _):
        place[owner[l]] = l
        return 0

    lax.fori_loop(0, OWNERS, invert, 0, unroll=8)

    def group_rows(s):
        return pl.ds(pl.multiple_of(s * (BLOCKS * RB), BLOCKS * RB), BLOCKS * RB)

    def copy_new(s):
        return pltpu.make_async_copy(new_v.at[group_rows(s)], expert_new.at[0, group_rows(s)], new_sem)

    def copy_codes(s):
        return pltpu.make_async_copy(codes_v.at[group_rows(s)], expert_codes.at[0, group_rows(s)], codes_sem)

    def group(s, _):
        for j in range(BLOCKS):
            rows = pl.ds(pl.multiple_of((s * BLOCKS + j) * RB, 8), RB)
            new_v[rows, :] = shadow[rows, :] + recv[place[s * BLOCKS + j]].astype(F32)
        copy_new(s).start()
        for j in range(TILES):
            i = s * TILES + j
            rows = pl.ds(pl.multiple_of(i * BLK, BLK), BLK)
            tile = new_v[rows, :]
            column = jnp.max(jnp.abs(tile), axis=0, keepdims=True)
            top = jnp.max(column, axis=1, keepdims=True)
            chosen = jnp.where(mode[i] == 0, jnp.broadcast_to(top, column.shape), column)
            amax_v[pl.ds(i, 1), :] = chosen
            codes_v[rows, :] = (tile * (1.0 / (chosen + 1e-6))).astype(BF16)
        copy_codes(s).start()
        return 0

    lax.fori_loop(0, SUPER, group, 0)
    copy_am = pltpu.make_async_copy(amax_v, expert_amax.at[0], out_sem.at[2])
    copy_am.start()
    copy_an.wait()
    copy_ac.wait()
    copy_am.wait()
    copy_aa.wait()
    pltpu.make_async_copy(new_v, expert_new.at[0], new_sem).wait()
    pltpu.make_async_copy(codes_v, expert_codes.at[0], codes_sem).wait()


def on_device(learner_delta, owner_block, expert_shadow, tile_mode, attn_delta, attn_shadow):
    vmem = pl.BlockSpec(memory_space=pltpu.VMEM)
    hbm = pl.BlockSpec(memory_space=pltpu.HBM)
    dma = pltpu.SemaphoreType.DMA
    shape = jax.ShapeDtypeStruct
    in_hbm = functools.partial(pltpu.with_memory_space_constraint, memory_space=pltpu.HBM)
    recv, shadow, att_new_v, att_codes_v, att_amax_v = pl.pallas_call(
        exchange,
        name="exchange",
        out_shape=(
            pltpu.VMEM((OWNERS, RB, BLK), BF16),
            pltpu.VMEM((ROWS, BLK), F32),
            pltpu.VMEM((64, 8, ATT_COLS), F32),
            pltpu.VMEM((512, ATT_COLS), BF16),
            pltpu.VMEM((4, BLK), F32),
        ),
        in_specs=[hbm] * 4,
        out_specs=(vmem,) * 5,
        scratch_shapes=[
            pltpu.VMEM((RB, EXPERTS, 1024), BF16),
            pltpu.VMEM((SHARES, RB * EXPERTS + EXPERTS, BLK), F32),
            pltpu.VMEM((OWNERS, RB, BLK), BF16),
            pltpu.VMEM((2, 4, 16, ATT_ROWS, ATT_COLS), BF16),
            pltpu.VMEM((64, 8, ATT_COLS), F32),
            pltpu.VMEM((64, 8, ATT_COLS), F32),
            dma((4,)), dma(()), dma(()), dma(()), dma(()),
            dma((2, 2)), dma((2, 2)), dma((2,)), dma((2,)), dma((5,)), dma((5,)),
        ],
        compiler_params=pltpu.CompilerParams(
            collective_id=0, has_side_effects=True, vmem_limit_bytes=40 << 20
        ),
    )(*(in_hbm(x) for x in (learner_delta, attn_delta, attn_shadow.reshape(64, 8, ATT_COLS), expert_shadow)))

    return pl.pallas_call(
        finish,
        name="finish",
        out_shape=(
            shape((1, ROWS, BLK), F32),
            shape((1, ROWS, BLK), BF16),
            shape((1, ROWS // BLK, BLK), F32),
            shape((512, ATT_COLS), F32),
            shape((512, ATT_COLS), BF16),
            shape((4, ATT_TILES), F32),
        ),
        in_specs=[vmem] * 7,
        out_specs=(hbm,) * 6,
        scratch_shapes=[
            pltpu.SMEM((OWNERS,), jnp.int32),
            pltpu.SMEM((ROWS // BLK,), jnp.int32),
            pltpu.SMEM((OWNERS,), jnp.int32),
            pltpu.VMEM((ROWS, BLK), F32),
            pltpu.VMEM((ROWS, BLK), BF16),
            pltpu.VMEM((ROWS // BLK, BLK), F32),
            pltpu.VMEM((4, ATT_TILES), F32),
            dma((6,)), dma(()), dma(()),
        ],
        compiler_params=pltpu.CompilerParams(vmem_limit_bytes=40 << 20),
    )(owner_block, tile_mode.reshape(ROWS // BLK), recv, shadow, att_new_v.reshape(512, ATT_COLS), att_codes_v, att_amax_v)


def solution(mesh):
    return jax.shard_map(
        on_device,
        mesh=mesh,
        in_specs=(
            P(("expert", "tensor"), None, None, None),
            P(),
            P("expert", None, "tensor"),
            P("expert", None, "tensor"),
            P(("expert", "tensor"), None),
            P(None, "tensor"),
        ),
        out_specs=(
            P("expert", None, "tensor"),
            P("expert", None, "tensor"),
            P("expert", None, "tensor"),
            P(None, "tensor"),
            P(None, "tensor"),
            P(None, "tensor"),
        ),
        check_vma=False,
    )
```

```python
import functools

import jax
import jax.numpy as jnp
from jax import lax
from jax.experimental import pallas as pl
from jax.experimental.pallas import tpu as pltpu
from jax.sharding import PartitionSpec as P

MESH = pl.DeviceIdType.MESH
BLK = 128
F32 = jnp.float32
BF16 = jnp.bfloat16

OWNERS = 128
RB = 56
EXPERTS = 16
SHARES = 8
ROWS = OWNERS * RB
ATT_ROWS = 4
ATT_COLS = 2048
ATT_TILES = ATT_COLS // BLK
SUPER = 8
BLOCKS = 16
TILES = 7


AHEAD, BETWEEN, UPTO = 45, 0, 127
STRIDE = 21


def exchange(
    delta, attn_delta, attn_shadow, expert_shadow,
    recv, shadow, attn_new, attn_codes, attn_amax,
    held, wide, send, gath, att_old, att_wide,
    load_sem, send_sem, recv_sem, first_send, first_recv, second_send, second_recv, third_send, third_recv,
    last_send, last_recv,
):
    e = lax.axis_index("expert")
    t = lax.axis_index("tensor")
    me = e * SHARES + t
    x, y, core = lax.div(e, 4), lax.rem(t, 4), lax.rem(e, 2)
    high, low = lax.div(t, 4), lax.rem(lax.div(e, 2), 2)
    z = high * 2 + low

    def step(v, d):
        return lax.rem(v + d, 4)

    def at(x, y, z, core):
        return x * 4 + lax.rem(z, 2) * 2 + core, lax.div(z, 2) * 4 + y

    load_delta = pltpu.make_async_copy(delta.at[0], held, load_sem.at[0])
    load_delta.start()

    to_x = [step(x, d) * 4 for d in range(4)]
    to_y = [step(y, d) for d in range(4)]
    to_z = [(lax.rem(step(z, d), 2) * 2, lax.div(step(z, d), 2) * 4) for d in range(4)]
    to_core = (core, 1 - core)
    barrier = pltpu.get_barrier_semaphore()
    for s in sorted(range(1, OWNERS), key=lambda s: -sum(min(d, 4 - d) for d in (s // 32, s // 8 % 4, s // 2 % 4))):
        near, far = to_z[s // 2 % 4]
        pl.semaphore_signal(
            barrier, inc=1, device_id=(to_x[s // 32] + near + to_core[s % 2], far + to_y[s // 8 % 4]), device_id_type=MESH
        )

    def columns(there, y):
        share = lax.div(there, 2) * 4 + y
        return attn_delta.at[:, pl.ds(pl.multiple_of(share * ATT_COLS, BLK), ATT_COLS)]

    mine = z * 4 + y
    own = pltpu.make_async_copy(columns(z, y), gath.at[core, x, mine], load_sem.at[1])
    own.start()
    load_att = pltpu.make_async_copy(attn_shadow, att_old, load_sem.at[2])
    load_att.start()
    load_exp = pltpu.make_async_copy(expert_shadow.at[0], shadow, load_sem.at[3])
    load_exp.start()

    load_delta.wait()

    def widen(r, _):
        rows = held[r].astype(F32)
        for j in range(SHARES):
            wide[j, pl.ds(pl.multiple_of(r * EXPERTS, EXPERTS), EXPERTS), :] = rows[:, j * BLK:(j + 1) * BLK]
        return 0

    lax.fori_loop(0, RB, widen, 0, unroll=2)

    def block_of(pe, pt):
        return wide[pt, pl.ds(pe, RB, stride=EXPERTS), :].astype(BF16)

    recv[me] = block_of(e, t)

    pl.semaphore_wait(barrier, OWNERS - 1)

    for k in (10, 5, 15, 7, 13, 2, 8, 9, 6, 11, 14, 1, 4, 3, 12):
        there, over = step(z, k // 4), step(y, k % 4)
        pltpu.make_async_remote_copy(
            src_ref=columns(there, over), dst_ref=gath.at[core, x, mine], send_sem=first_send, recv_sem=first_recv,
            device_id=at(x, over, there, core), device_id_type=MESH,
        ).start()

    def send_block(k, _):
        s = lax.rem(k * STRIDE, 32)
        dx = jnp.where(k <= 32, 2, jnp.where(k <= 64, 1, jnp.where(k <= 96, 3, 0)))
        dy, dz = lax.div(s, 8), lax.rem(lax.div(s, 2), 4)
        pe, pt = at(step(x, dx), step(y, dy), step(z, dz), lax.rem(core + s, 2))
        p = pe * SHARES + pt
        send[p] = block_of(pe, pt)
        pltpu.make_async_remote_copy(
            src_ref=send.at[p],
            dst_ref=recv.at[me],
            send_sem=send_sem,
            recv_sem=recv_sem,
            device_id=(pe, pt),
            device_id_type=MESH,
        ).start()
        return 0

    lax.fori_loop(1, AHEAD, send_block, 0)

    own.wait()
    landed = gath.at[0, 0, pl.ds(0, 15)]
    pltpu.make_async_copy(landed, landed, first_recv).wait()

    sides = (1, 3)

    def half(h):
        return pl.ds(8 * h, 8)

    def hand(i, rows, to, sent, got):
        ref = gath.at[core, i, rows]
        return pltpu.make_async_remote_copy(
            src_ref=ref, dst_ref=ref, send_sem=sent, recv_sem=got, device_id=to, device_id_type=MESH
        )

    def beside(n, h):
        return hand(x, half(h), at(step(x, sides[n]), y, z, core), second_send.at[n, h], second_recv.at[n, h])

    def onward(n):
        return hand(
            step(x, 4 - sides[n]), half(n), at(step(x, sides[n]), y, z, core), third_send.at[n], third_recv.at[n]
        )

    def across(n):
        i, rows = ((0, pl.ds(0, 16)), (3, pl.ds(0, 16)), (1, pl.ds(0, 16)), (2, half(0)), (2, half(1)))[n]
        return hand(step(x, i), rows, at(x, y, z, 1 - core), last_send.at[n], last_recv.at[n])

    k = AHEAD
    for start in (
        beside(0, 0).start, beside(1, 1).start, beside(0, 1).start, beside(1, 0).start, across(0).start
    ):
        start()
        lax.fori_loop(k, k + BETWEEN, send_block, 0)
        k += BETWEEN
    lax.fori_loop(k, UPTO, send_block, 0)
    for n in range(2):
        beside(n, n).wait_recv()
        onward(n).start()
    lax.fori_loop(UPTO, OWNERS, send_block, 0)

    def att_widen(m, _):
        i, j = lax.div(m, 4), lax.rem(m, 4)
        gx, gc = lax.div(i, 4), lax.rem(i, 2)
        gz = lax.div(j, 2) * 2 + lax.rem(lax.div(i, 2), 2)
        for n in range(2):
            owner = gz * 4 + lax.rem(j, 2) * 2 + n
            rows = slice(4 * n, 4 * n + 4)
            att_wide[m, rows, :] = gath[gc, gx, owner].astype(F32)
        return 0

    def att_tile_row(i, _):
        tops = []
        for j in range(ATT_TILES):
            cols = slice(j * BLK, (j + 1) * BLK)
            groups = pl.ds(i * 16, 16)
            new = att_old[groups, :, cols] + att_wide[groups, :, cols]
            attn_new[groups, :, cols] = new
            top = jnp.max(jnp.max(jnp.max(jnp.abs(new), axis=0), axis=0, keepdims=True), axis=1, keepdims=True)
            codes = new * (1.0 / (top + 1e-6))[None]
            attn_codes[pl.ds(pl.multiple_of(i * BLK, BLK), BLK), cols] = codes.reshape(BLK, BLK).astype(BF16)
            tops.append(jnp.broadcast_to(top, (1, BLK)))
        lane = lax.broadcasted_iota(jnp.int32, (1, BLK), 1)
        row = jnp.zeros((1, BLK), F32)
        for j in range(ATT_TILES):
            row = jnp.where(lane == j, tops[j], row)
        attn_amax[pl.ds(i, 1), :] = row
        return 0

    load_att.wait()

    def work(r):
        i = step(x, r)
        lax.fori_loop(i * 16, i * 16 + 16, att_widen, 0)
        att_tile_row(i, 0)

    across(0).wait_recv()
    work(0)
    for n in range(2):
        beside(n, 1 - n).wait_recv()
        across(1 + n).start()
    for n in range(2):
        across(1 + n).wait_recv()
        work((3, 1)[n])
    for n in range(2):
        onward(n).wait_recv()
        across(3 + n).start()
    for n in range(2):
        across(3 + n).wait_recv()
    work(2)

    load_exp.wait()
    pltpu.make_async_copy(landed, landed, first_send).wait()
    for n in range(2):
        beside(n, 0).wait_send()
        beside(n, 1).wait_send()
        onward(n).wait_send()
    for n in range(5):
        across(n).wait_send()
    whole = pl.ds(0, OWNERS - 1)
    pltpu.make_async_copy(send.at[whole], send.at[whole], send_sem).wait()
    pltpu.make_async_copy(recv.at[whole], recv.at[whole], recv_sem).wait()


def finish(
    owner_v, mode_v, recv, shadow, att_new_v, att_codes_v, att_amax_v,
    expert_new, expert_codes, expert_amax, attn_new, attn_codes, attn_amax,
    owner, mode, place, new_v, codes_v, amax_v, att_small, out_sem, new_sem, codes_sem,
):
    copy_an = pltpu.make_async_copy(att_new_v, attn_new, out_sem.at[0])
    copy_ac = pltpu.make_async_copy(att_codes_v, attn_codes, out_sem.at[1])

    copy_owner = pltpu.make_async_copy(owner_v, owner, out_sem.at[4])
    copy_mode = pltpu.make_async_copy(mode_v, mode, out_sem.at[5])
    copy_owner.start()
    copy_mode.start()
    copy_an.start()
    copy_ac.start()
    att_small[...] = att_amax_v[:, :ATT_TILES]
    copy_aa = pltpu.make_async_copy(att_small, attn_amax, out_sem.at[3])
    copy_aa.start()
    copy_owner.wait()
    copy_mode.wait()

    def invert(l, _):
        place[owner[l]] = l
        return 0

    lax.fori_loop(0, OWNERS, invert, 0, unroll=8)

    def group_rows(s):
        return pl.ds(pl.multiple_of(s * (BLOCKS * RB), BLOCKS * RB), BLOCKS * RB)

    def copy_new(s):
        return pltpu.make_async_copy(new_v.at[group_rows(s)], expert_new.at[0, group_rows(s)], new_sem)

    def copy_codes(s):
        return pltpu.make_async_copy(codes_v.at[group_rows(s)], expert_codes.at[0, group_rows(s)], codes_sem)

    def group(s, _):
        for j in range(BLOCKS):
            rows = pl.ds(pl.multiple_of((s * BLOCKS + j) * RB, 8), RB)
            new_v[rows, :] = shadow[rows, :] + recv[place[s * BLOCKS + j]].astype(F32)
        copy_new(s).start()
        for j in range(TILES):
            i = s * TILES + j
            rows = pl.ds(pl.multiple_of(i * BLK, BLK), BLK)
            tile = new_v[rows, :]
            column = jnp.max(jnp.abs(tile), axis=0, keepdims=True)
            top = jnp.max(column, axis=1, keepdims=True)
            chosen = jnp.where(mode[i] == 0, jnp.broadcast_to(top, column.shape), column)
            amax_v[pl.ds(i, 1), :] = chosen
            codes_v[rows, :] = (tile * (1.0 / (chosen + 1e-6))).astype(BF16)
        copy_codes(s).start()
        return 0

    lax.fori_loop(0, SUPER, group, 0)
    copy_am = pltpu.make_async_copy(amax_v, expert_amax.at[0], out_sem.at[2])
    copy_am.start()
    copy_an.wait()
    copy_ac.wait()
    copy_am.wait()
    copy_aa.wait()
    pltpu.make_async_copy(new_v, expert_new.at[0], new_sem).wait()
    pltpu.make_async_copy(codes_v, expert_codes.at[0], codes_sem).wait()


def on_device(learner_delta, owner_block, expert_shadow, tile_mode, attn_delta, attn_shadow):
    vmem = pl.BlockSpec(memory_space=pltpu.VMEM)
    hbm = pl.BlockSpec(memory_space=pltpu.HBM)
    dma = pltpu.SemaphoreType.DMA
    shape = jax.ShapeDtypeStruct
    in_hbm = functools.partial(pltpu.with_memory_space_constraint, memory_space=pltpu.HBM)
    recv, shadow, att_new_v, att_codes_v, att_amax_v = pl.pallas_call(
        exchange,
        name="exchange",
        out_shape=(
            pltpu.VMEM((OWNERS, RB, BLK), BF16),
            pltpu.VMEM((ROWS, BLK), F32),
            pltpu.VMEM((64, 8, ATT_COLS), F32),
            pltpu.VMEM((512, ATT_COLS), BF16),
            pltpu.VMEM((4, BLK), F32),
        ),
        in_specs=[hbm] * 4,
        out_specs=(vmem,) * 5,
        scratch_shapes=[
            pltpu.VMEM((RB, EXPERTS, 1024), BF16),
            pltpu.VMEM((SHARES, RB * EXPERTS + EXPERTS, BLK), F32),
            pltpu.VMEM((OWNERS, RB, BLK), BF16),
            pltpu.VMEM((2, 4, 16, ATT_ROWS, ATT_COLS), BF16),
            pltpu.VMEM((64, 8, ATT_COLS), F32),
            pltpu.VMEM((64, 8, ATT_COLS), F32),
            dma((4,)), dma(()), dma(()), dma(()), dma(()),
            dma((2, 2)), dma((2, 2)), dma((2,)), dma((2,)), dma((5,)), dma((5,)),
        ],
        compiler_params=pltpu.CompilerParams(
            collective_id=0, has_side_effects=True, vmem_limit_bytes=40 << 20
        ),
    )(*(in_hbm(x) for x in (learner_delta, attn_delta, attn_shadow.reshape(64, 8, ATT_COLS), expert_shadow)))

    return pl.pallas_call(
        finish,
        name="finish",
        out_shape=(
            shape((1, ROWS, BLK), F32),
            shape((1, ROWS, BLK), BF16),
            shape((1, ROWS // BLK, BLK), F32),
            shape((512, ATT_COLS), F32),
            shape((512, ATT_COLS), BF16),
            shape((4, ATT_TILES), F32),
        ),
        in_specs=[vmem] * 7,
        out_specs=(hbm,) * 6,
        scratch_shapes=[
            pltpu.SMEM((OWNERS,), jnp.int32),
            pltpu.SMEM((ROWS // BLK,), jnp.int32),
            pltpu.SMEM((OWNERS,), jnp.int32),
            pltpu.VMEM((ROWS, BLK), F32),
            pltpu.VMEM((ROWS, BLK), BF16),
            pltpu.VMEM((ROWS // BLK, BLK), F32),
            pltpu.VMEM((4, ATT_TILES), F32),
            dma((6,)), dma(()), dma(()),
        ],
        compiler_params=pltpu.CompilerParams(vmem_limit_bytes=40 << 20),
    )(owner_block, tile_mode.reshape(ROWS // BLK), recv, shadow, att_new_v.reshape(512, ATT_COLS), att_codes_v, att_amax_v)


def solution(mesh):
    return jax.shard_map(
        on_device,
        mesh=mesh,
        in_specs=(
            P(("expert", "tensor"), None, None, None),
            P(),
            P("expert", None, "tensor"),
            P("expert", None, "tensor"),
            P(("expert", "tensor"), None),
            P(None, "tensor"),
        ),
        out_specs=(
            P("expert", None, "tensor"),
            P("expert", None, "tensor"),
            P("expert", None, "tensor"),
            P(None, "tensor"),
            P(None, "tensor"),
            P(None, "tensor"),
        ),
        check_vma=False,
    )
```

```python
import functools

import jax
import jax.numpy as jnp
from jax import lax
from jax.experimental import pallas as pl
from jax.experimental.pallas import tpu as pltpu
from jax.sharding import PartitionSpec as P

MESH = pl.DeviceIdType.MESH
BLK = 128
F32 = jnp.float32
BF16 = jnp.bfloat16

OWNERS = 128
RB = 56
EXPERTS = 16
SHARES = 8
ROWS = OWNERS * RB
ATT_ROWS = 4
ATT_COLS = 2048
ATT_TILES = ATT_COLS // BLK
SUPER = 8
BLOCKS = 16
TILES = 7


AHEAD, LATER, BETWEEN = 30, 65, 2
STRIDE = 21


def exchange(
    delta, attn_delta, attn_shadow, expert_shadow,
    recv, shadow, attn_new, attn_codes, attn_amax,
    held, wide, send, gath, att_old, att_wide,
    load_sem, send_sem, recv_sem, first_send, first_recv, second_send, second_recv, third_send, third_recv,
    last_send, last_recv,
):
    e = lax.axis_index("expert")
    t = lax.axis_index("tensor")
    me = e * SHARES + t
    x, y, core = lax.div(e, 4), lax.rem(t, 4), lax.rem(e, 2)
    high, low = lax.div(t, 4), lax.rem(lax.div(e, 2), 2)
    z = high * 2 + low

    def step(v, d):
        return lax.rem(v + d, 4)

    def at(x, y, z, core):
        return x * 4 + lax.rem(z, 2) * 2 + core, lax.div(z, 2) * 4 + y

    load_delta = pltpu.make_async_copy(delta.at[0], held, load_sem.at[0])
    load_delta.start()

    to_x = [step(x, d) * 4 for d in range(4)]
    to_y = [step(y, d) for d in range(4)]
    to_z = [(lax.rem(step(z, d), 2) * 2, lax.div(step(z, d), 2) * 4) for d in range(4)]
    to_core = (core, 1 - core)
    barrier = pltpu.get_barrier_semaphore()
    for s in sorted(range(1, OWNERS), key=lambda s: -sum(min(d, 4 - d) for d in (s // 32, s // 8 % 4, s // 2 % 4))):
        near, far = to_z[s // 2 % 4]
        pl.semaphore_signal(
            barrier, inc=1, device_id=(to_x[s // 32] + near + to_core[s % 2], far + to_y[s // 8 % 4]), device_id_type=MESH
        )

    def columns(there, y):
        share = lax.div(there, 2) * 4 + y
        return attn_delta.at[:, pl.ds(pl.multiple_of(share * ATT_COLS, BLK), ATT_COLS)]

    mine = z * 4 + y
    own = pltpu.make_async_copy(columns(z, y), gath.at[core, x, mine], load_sem.at[1])
    own.start()
    load_att = pltpu.make_async_copy(attn_shadow, att_old, load_sem.at[2])
    load_att.start()
    load_exp = pltpu.make_async_copy(expert_shadow.at[0], shadow, load_sem.at[3])
    load_exp.start()

    load_delta.wait()

    def widen(r, _):
        rows = held[r].astype(F32)
        for j in range(SHARES):
            wide[j, pl.ds(pl.multiple_of(r * EXPERTS, EXPERTS), EXPERTS), :] = rows[:, j * BLK:(j + 1) * BLK]
        return 0

    lax.fori_loop(0, RB, widen, 0, unroll=2)

    def block_of(pe, pt):
        return wide[pt, pl.ds(pe, RB, stride=EXPERTS), :].astype(BF16)

    recv[me] = block_of(e, t)

    pl.semaphore_wait(barrier, OWNERS - 1)

    for k in (2, 5, 7, 6, 1, 4, 3, 10, 15, 13, 8, 9, 11, 14, 12):
        there, over = step(z, k // 4), step(y, k % 4)
        pltpu.make_async_remote_copy(
            src_ref=columns(there, over), dst_ref=gath.at[core, x, mine], send_sem=first_send.at[k // 8], recv_sem=first_recv.at[k // 8],
            device_id=at(x, over, there, core), device_id_type=MESH,
        ).start()

    def send_block(k, _):
        s = lax.rem(k * STRIDE, 32)
        dx = jnp.where(k <= 32, 2, jnp.where(k <= 64, 1, jnp.where(k <= 96, 3, 0)))
        dy, dz = lax.div(s, 8), lax.rem(lax.div(s, 2), 4)
        pe, pt = at(step(x, dx), step(y, dy), step(z, dz), lax.rem(core + s, 2))
        p = pe * SHARES + pt
        send[p] = block_of(pe, pt)
        pltpu.make_async_remote_copy(
            src_ref=send.at[p],
            dst_ref=recv.at[me],
            send_sem=send_sem,
            recv_sem=recv_sem,
            device_id=(pe, pt),
            device_id_type=MESH,
        ).start()
        return 0

    lax.fori_loop(1, AHEAD, send_block, 0)

    own.wait()
    landed = (gath.at[0, 0, pl.ds(0, 7)], gath.at[0, 0, pl.ds(0, 8)])
    pltpu.make_async_copy(landed[0], landed[0], first_recv.at[0]).wait()

    sides = (1, 3)

    def quarter(q):
        return pl.ds(step(z, 4 - q) * 4, 4)

    def hand(i, rows, to, sent, got):
        ref = gath.at[core, i, rows]
        return pltpu.make_async_remote_copy(
            src_ref=ref, dst_ref=ref, send_sem=sent, recv_sem=got, device_id=to, device_id_type=MESH
        )

    def beside(n, q):
        to = at(step(x, sides[n]), y, z, core)
        return hand(x, quarter(q), to, second_send.at[n, q], second_recv.at[n, q])

    def onward(n, q):
        to = at(step(x, sides[n]), y, z, core)
        return hand(step(x, 4 - sides[n]), quarter(q), to, third_send.at[q], third_recv.at[q])

    def across(n):
        return hand(step(x, (0, 3, 1, 2)[n]), pl.ds(0, 16), at(x, y, z, 1 - core), last_send.at[n], last_recv.at[n])

    k = AHEAD
    for n, q in ((0, 0), (1, 1), (0, 1), (1, 0)):
        beside(n, q).start()
        lax.fori_loop(k, k + BETWEEN, send_block, 0)
        k += BETWEEN
    lax.fori_loop(k, LATER, send_block, 0)
    pltpu.make_async_copy(landed[1], landed[1], first_recv.at[1]).wait()
    k = LATER
    for n, q in ((1, 2), (0, 3), (1, 3), (0, 2)):
        beside(n, q).start()
        lax.fori_loop(k, k + BETWEEN, send_block, 0)
        k += BETWEEN
    across(0).start()
    lax.fori_loop(k, OWNERS - 1, send_block, 0)
    for q in range(4):
        beside(q // 2, q).wait_recv()
        onward(q // 2, q).start()
    lax.fori_loop(OWNERS - 1, OWNERS, send_block, 0)

    def att_widen(m, _):
        i, j = lax.div(m, 4), lax.rem(m, 4)
        gx, gc = lax.div(i, 4), lax.rem(i, 2)
        gz = lax.div(j, 2) * 2 + lax.rem(lax.div(i, 2), 2)
        for n in range(2):
            owner = gz * 4 + lax.rem(j, 2) * 2 + n
            rows = slice(4 * n, 4 * n + 4)
            att_wide[m, rows, :] = gath[gc, gx, owner].astype(F32)
        return 0

    def att_tile_row(i, _):
        tops = []
        for j in range(ATT_TILES):
            cols = slice(j * BLK, (j + 1) * BLK)
            groups = pl.ds(i * 16, 16)
            new = att_old[groups, :, cols] + att_wide[groups, :, cols]
            attn_new[groups, :, cols] = new
            top = jnp.max(jnp.max(jnp.max(jnp.abs(new), axis=0), axis=0, keepdims=True), axis=1, keepdims=True)
            codes = new * (1.0 / (top + 1e-6))[None]
            attn_codes[pl.ds(pl.multiple_of(i * BLK, BLK), BLK), cols] = codes.reshape(BLK, BLK).astype(BF16)
            tops.append(jnp.broadcast_to(top, (1, BLK)))
        lane = lax.broadcasted_iota(jnp.int32, (1, BLK), 1)
        row = jnp.zeros((1, BLK), F32)
        for j in range(ATT_TILES):
            row = jnp.where(lane == j, tops[j], row)
        attn_amax[pl.ds(i, 1), :] = row
        return 0

    load_att.wait()

    def work(r):
        i = step(x, r)
        lax.fori_loop(i * 16, i * 16 + 16, att_widen, 0)
        att_tile_row(i, 0)

    across(0).wait_recv()
    work(0)
    for n in range(2):
        for q in (2 - 2 * n, 3 - 2 * n):
            beside(n, q).wait_recv()
        across(1 + n).start()
    for n in range(2):
        across(1 + n).wait_recv()
        work((3, 1)[n])
    for q in range(4):
        onward(q // 2, q).wait_recv()
    across(3).start()
    across(3).wait_recv()
    work(2)

    load_exp.wait()
    for n in range(2):
        pltpu.make_async_copy(landed[n], landed[n], first_send.at[n]).wait()
        for q in range(4):
            beside(n, q).wait_send()
    for q in range(4):
        onward(q // 2, q).wait_send()
        across(q).wait_send()
    whole = pl.ds(0, OWNERS - 1)
    pltpu.make_async_copy(send.at[whole], send.at[whole], send_sem).wait()
    pltpu.make_async_copy(recv.at[whole], recv.at[whole], recv_sem).wait()


def finish(
    owner_v, mode_v, recv, shadow, att_new_v, att_codes_v, att_amax_v,
    expert_new, expert_codes, expert_amax, attn_new, attn_codes, attn_amax,
    owner, mode, place, new_v, codes_v, amax_v, att_small, out_sem, new_sem, codes_sem,
):
    copy_an = pltpu.make_async_copy(att_new_v, attn_new, out_sem.at[0])
    copy_ac = pltpu.make_async_copy(att_codes_v, attn_codes, out_sem.at[1])

    copy_owner = pltpu.make_async_copy(owner_v, owner, out_sem.at[4])
    copy_mode = pltpu.make_async_copy(mode_v, mode, out_sem.at[5])
    copy_owner.start()
    copy_mode.start()
    copy_an.start()
    copy_ac.start()
    att_small[...] = att_amax_v[:, :ATT_TILES]
    copy_aa = pltpu.make_async_copy(att_small, attn_amax, out_sem.at[3])
    copy_aa.start()
    copy_owner.wait()
    copy_mode.wait()

    def invert(l, _):
        place[owner[l]] = l
        return 0

    lax.fori_loop(0, OWNERS, invert, 0, unroll=8)

    def group_rows(s):
        return pl.ds(pl.multiple_of(s * (BLOCKS * RB), BLOCKS * RB), BLOCKS * RB)

    def copy_new(s):
        return pltpu.make_async_copy(new_v.at[group_rows(s)], expert_new.at[0, group_rows(s)], new_sem)

    def copy_codes(s):
        return pltpu.make_async_copy(codes_v.at[group_rows(s)], expert_codes.at[0, group_rows(s)], codes_sem)

    def group(s, _):
        for j in range(BLOCKS):
            rows = pl.ds(pl.multiple_of((s * BLOCKS + j) * RB, 8), RB)
            new_v[rows, :] = shadow[rows, :] + recv[place[s * BLOCKS + j]].astype(F32)
        copy_new(s).start()
        for j in range(TILES):
            i = s * TILES + j
            rows = pl.ds(pl.multiple_of(i * BLK, BLK), BLK)
            tile = new_v[rows, :]
            column = jnp.max(jnp.abs(tile), axis=0, keepdims=True)
            top = jnp.max(column, axis=1, keepdims=True)
            chosen = jnp.where(mode[i] == 0, jnp.broadcast_to(top, column.shape), column)
            amax_v[pl.ds(i, 1), :] = chosen
            codes_v[rows, :] = (tile * (1.0 / (chosen + 1e-6))).astype(BF16)
        copy_codes(s).start()
        return 0

    lax.fori_loop(0, SUPER, group, 0)
    copy_am = pltpu.make_async_copy(amax_v, expert_amax.at[0], out_sem.at[2])
    copy_am.start()
    copy_an.wait()
    copy_ac.wait()
    copy_am.wait()
    copy_aa.wait()
    pltpu.make_async_copy(new_v, expert_new.at[0], new_sem).wait()
    pltpu.make_async_copy(codes_v, expert_codes.at[0], codes_sem).wait()


def on_device(learner_delta, owner_block, expert_shadow, tile_mode, attn_delta, attn_shadow):
    vmem = pl.BlockSpec(memory_space=pltpu.VMEM)
    hbm = pl.BlockSpec(memory_space=pltpu.HBM)
    dma = pltpu.SemaphoreType.DMA
    shape = jax.ShapeDtypeStruct
    in_hbm = functools.partial(pltpu.with_memory_space_constraint, memory_space=pltpu.HBM)
    recv, shadow, att_new_v, att_codes_v, att_amax_v = pl.pallas_call(
        exchange,
        name="exchange",
        out_shape=(
            pltpu.VMEM((OWNERS, RB, BLK), BF16),
            pltpu.VMEM((ROWS, BLK), F32),
            pltpu.VMEM((64, 8, ATT_COLS), F32),
            pltpu.VMEM((512, ATT_COLS), BF16),
            pltpu.VMEM((4, BLK), F32),
        ),
        in_specs=[hbm] * 4,
        out_specs=(vmem,) * 5,
        scratch_shapes=[
            pltpu.VMEM((RB, EXPERTS, 1024), BF16),
            pltpu.VMEM((SHARES, RB * EXPERTS + EXPERTS, BLK), F32),
            pltpu.VMEM((OWNERS, RB, BLK), BF16),
            pltpu.VMEM((2, 4, 16, ATT_ROWS, ATT_COLS), BF16),
            pltpu.VMEM((64, 8, ATT_COLS), F32),
            pltpu.VMEM((64, 8, ATT_COLS), F32),
            dma((4,)), dma(()), dma(()), dma((2,)), dma((2,)),
            dma((2, 4)), dma((2, 4)), dma((4,)), dma((4,)), dma((4,)), dma((4,)),
        ],
        compiler_params=pltpu.CompilerParams(
            collective_id=0, has_side_effects=True, vmem_limit_bytes=40 << 20
        ),
    )(*(in_hbm(x) for x in (learner_delta, attn_delta, attn_shadow.reshape(64, 8, ATT_COLS), expert_shadow)))

    return pl.pallas_call(
        finish,
        name="finish",
        out_shape=(
            shape((1, ROWS, BLK), F32),
            shape((1, ROWS, BLK), BF16),
            shape((1, ROWS // BLK, BLK), F32),
            shape((512, ATT_COLS), F32),
            shape((512, ATT_COLS), BF16),
            shape((4, ATT_TILES), F32),
        ),
        in_specs=[vmem] * 7,
        out_specs=(hbm,) * 6,
        scratch_shapes=[
            pltpu.SMEM((OWNERS,), jnp.int32),
            pltpu.SMEM((ROWS // BLK,), jnp.int32),
            pltpu.SMEM((OWNERS,), jnp.int32),
            pltpu.VMEM((ROWS, BLK), F32),
            pltpu.VMEM((ROWS, BLK), BF16),
            pltpu.VMEM((ROWS // BLK, BLK), F32),
            pltpu.VMEM((4, ATT_TILES), F32),
            dma((6,)), dma(()), dma(()),
        ],
        compiler_params=pltpu.CompilerParams(vmem_limit_bytes=40 << 20),
    )(owner_block, tile_mode.reshape(ROWS // BLK), recv, shadow, att_new_v.reshape(512, ATT_COLS), att_codes_v, att_amax_v)


def solution(mesh):
    return jax.shard_map(
        on_device,
        mesh=mesh,
        in_specs=(
            P(("expert", "tensor"), None, None, None),
            P(),
            P("expert", None, "tensor"),
            P("expert", None, "tensor"),
            P(("expert", "tensor"), None),
            P(None, "tensor"),
        ),
        out_specs=(
            P("expert", None, "tensor"),
            P("expert", None, "tensor"),
            P("expert", None, "tensor"),
            P(None, "tensor"),
            P(None, "tensor"),
            P(None, "tensor"),
        ),
        check_vma=False,
    )
```
